32 devices in a mesh: grp: 2 (over y), gx: 8 (over z, x), gy: 2 (over core).
Axes of the slice: x: 2, y: 2, z: 4, core: 2. Of those that a mesh axis runs over, the one named last changes fastest.
Arguments:
- tokens: bfloat16 [2, 16, 8192], P(None, ('grp', 'gx'), 'gy'), parts along dimension 1, may hold values from -2000 to 2000, as said below
- norm_gain: float32 [8192], P('gy'), may hold values from 0.1 to 1.9
- gate_weight: bfloat16 [8192, 26624], P('gy', 'gx'), may hold values from -0.0625 to 0.0625
- up_weight: bfloat16 [8192, 26624], P('gy', 'gx'), may hold values from -0.0625 to 0.0625
- down_weight: bfloat16 [26624, 8192], P('gx', 'gy'), may hold values from -0.0390625 to 0.0390625
Outputs:
- block_out: bfloat16 [2, 16, 8192], P(None, ('grp', 'gx'), 'gy'), parts along dimension 1
The draws below stay inside these ranges and needn't reach their ends.
There are 2 independent parts, one for each index of `grp`. The reference program is written for one: setup_inputs(seed, part) draws one part's arguments, and reference() takes and returns one part's arrays. A program takes and returns all parts, laid end to end along the dimension named above; an argument that names none is the same for every part. Nothing has to cross between parts.
Inputs may be any that keep to these rules, and one draw needn't show every extreme that they name: `tokens`: hidden states of moderate size whose rows and features have unequal scales.
All inputs are finite; a program needn't handle non-finite values.
Results may differ from the reference program's by a relative error of at most 0.0065.
Values may be sent and summed in bfloat16 or wider, within the bound.
No kernel may reach another device: no remote copies, remote signals or barrier semaphores. Data moves between devices by JAX's collectives and lax.ppermute only.
A program may use at most 192 MiB of HBM per device.

```python
import jax
import jax.numpy as jnp
from jax import lax

D = 8192
FF = 26624
STEPS = 2
ROWS = 8


def draw_tokens(key, part):
    key = jax.random.fold_in(key, 11)
    key_base, key_cols, key_rows = jax.random.split(key, 3)
    ramp = 3.0 ** (jnp.arange(D, dtype=jnp.float32) / D)
    column_scale = jnp.exp(jax.random.uniform(key_cols, (D,), jnp.float32) * jnp.log(10.0))
    row_scale = jnp.exp(jax.random.uniform(key_rows, (STEPS, ROWS, 1), jnp.float32) * jnp.log(10.0))
    base = jnp.clip(jax.random.normal(key_base, (STEPS, ROWS, D), jnp.float32), -4.0, 4.0)
    return (base * row_scale * column_scale * ramp).astype(jnp.bfloat16)


def shard_levels(stream_key, dims, shards, low, largest):
    loudness = 1.0
    for dim, shards_of in shards:
        draws = jax.random.uniform(jax.random.fold_in(jax.random.fold_in(stream_key, 6), dim), (shards_of,), jnp.float32, low / len(shards), largest / len(shards))
        loudness = loudness * jnp.repeat(jnp.exp(draws), dims[dim] // shards_of).reshape((-1,) + (1,) * (len(dims) - 1 - dim))
    return loudness


def gaussian(own_key, shape, deviation, bound, pieces=(), kind=jnp.bfloat16):
    factor_of = shard_levels(own_key, shape, pieces, -0.22, 0.18) if pieces else 1.0
    array = jax.random.normal(own_key, shape, jnp.float32) * deviation * factor_of
    return jnp.minimum(jnp.maximum(array, -bound), bound).astype(kind)


def setup_inputs(seed: int = 0, part: int = 0) -> dict:
    keys = jax.random.split(jax.random.key(seed), 6)
    own_keys = jax.random.split(jax.random.fold_in(keys[5], part), 6)
    tokens = draw_tokens(jax.random.fold_in(jax.random.fold_in(keys[5], part), 71), part)
    norm_gain = jnp.clip(1.0 + 0.18 * jax.random.normal(keys[1], (D,), jnp.float32), 0.1, 1.9)
    gate_weight = gaussian(keys[2], (D, FF), D ** -0.5, 0.0625, ((0, 2), (1, 8)))
    up_weight = gaussian(keys[3], (D, FF), D ** -0.5, 0.0625, ((0, 2), (1, 8)))
    down_weight = gaussian(keys[4], (FF, D), FF ** -0.5, 0.0390625, ((0, 8), (1, 2)))
    return dict(tokens=tokens, norm_gain=norm_gain, gate_weight=gate_weight, up_weight=up_weight, down_weight=down_weight)


def reference(tokens, norm_gain, gate_weight, up_weight, down_weight):
    widened = tokens.astype(jnp.float32)
    mean_square = lax.optimization_barrier(jnp.sum(widened * widened, axis=2, keepdims=True)) / D
    normed = (widened * lax.rsqrt(mean_square + 1e-05) * norm_gain).astype(jnp.bfloat16)
    flattened = normed.reshape(STEPS * ROWS, D)
    gate_proj = jnp.dot(flattened, gate_weight, preferred_element_type=jnp.float32)
    up_proj = jnp.dot(flattened, up_weight, preferred_element_type=jnp.float32)
    hidden = (jax.nn.silu(gate_proj) * up_proj).astype(jnp.bfloat16)
    output_rows = jnp.dot(hidden, down_weight, preferred_element_type=jnp.float32).astype(jnp.bfloat16)
    return output_rows.reshape(STEPS, ROWS, D)
```

```python
import functools

import jax
import jax.numpy as jnp
from jax import lax
from jax.experimental import pallas as pl
from jax.experimental.pallas import tpu as pltpu
from jax.sharding import PartitionSpec as P

epsilon = 1e-05
f32, bf16 = jnp.float32, jnp.bfloat16
MiB = 2**20
VMEM = pl.BlockSpec(memory_space=pltpu.VMEM)
HBM = pl.BlockSpec(memory_space=pl.ANY)
Shape = jax.ShapeDtypeStruct

PAD = (512, 1024)
PADS = 32


def call(kernel, outs, *args, pads=(), specs=None, scratch=(), limit=2):
    skip = len(pads)
    specs = specs or [VMEM] * len(args)
    return pl.pallas_call(
        lambda *refs: kernel(*refs[skip:]),
        out_shape=outs,
        in_specs=[VMEM] * skip + specs,
        out_specs=jax.tree.map(lambda _: VMEM, outs),
        scratch_shapes=scratch,
        compiler_params=pltpu.CompilerParams(vmem_limit_bytes=limit * MiB),
    )(*pads, *args)


def empty_kernel(out_ref):
    pass


def squares_kernel(x_ref, sums_ref):
    x = x_ref[...].astype(f32)
    sums_ref[...] = jnp.broadcast_to(jnp.sum(x * x, axis=1, keepdims=True), sums_ref.shape)


def norm_kernel(width, x_ref, own_ref, other_ref, gain_ref, out_ref):
    mean_square = (own_ref[:, :1] + other_ref[:, :1]) / width
    x = x_ref[...].astype(f32)
    out_ref[...] = (x * lax.rsqrt(mean_square + epsilon) * gain_ref[...]).astype(bf16)


def join_kernel(first_ref, second_ref, out_ref):
    rows = first_ref.shape[0]
    out_ref[:rows, :] = first_ref[...]
    out_ref[rows:, :] = second_ref[...]


def project_kernel(x_ref, w_ref, out_ref):
    columns = w_ref.shape[1]
    for c in range(0, columns, 256):
        e = min(c + 256, columns)
        out_ref[:, c:e] = jnp.dot(x_ref[...], w_ref[:, c:e], preferred_element_type=f32)


def down_kernel(chunk, slots, g_ref, g2_ref, u_ref, u2_ref, w_ref, keep_ref, send_ref, acc_ref, h_ref, buf_ref, sems):
    units, width = w_ref.shape
    count = units // chunk

    def copy(k):
        return pltpu.make_async_copy(
            w_ref.at[pl.ds(k * chunk, chunk), :], buf_ref.at[k % slots], sems.at[k % slots]
        )

    for k in range(min(slots, count)):
        copy(k).start()
    v = g_ref[...] + g2_ref[...]
    h_ref[...] = (v / (1.0 + jnp.exp(-v)) * (u_ref[...] + u2_ref[...])).astype(bf16)
    for k in range(count):
        copy(k).wait()
        h = h_ref[:, k * chunk : (k + 1) * chunk]
        for c in range(0, width, 512):
            part = jnp.dot(h, buf_ref[k % slots, :, c : c + 512], preferred_element_type=f32)
            acc_ref[:, c : c + 512] = part if k == 0 else acc_ref[:, c : c + 512] + part
        if k + slots < count:
            copy(k + slots).start()
    rows = keep_ref.shape[0]
    keep_ref[...] = acc_ref[:rows, :]
    send_ref[...] = acc_ref[rows:, :]


def add_kernel(a_ref, b_ref, keep_ref, send_ref):
    rows = keep_ref.shape[0]
    total = a_ref[...] + b_ref[...]
    keep_ref[...] = total[:rows]
    send_ref[...] = total[rows:]


def last_kernel(a_ref, b_ref, out_ref):
    out_ref[...] = (a_ref[...] + b_ref[...]).astype(bf16)


def swap(x, axis, size, mask):
    return lax.ppermute(x, axis, [(i, i ^ mask) for i in range(size)])


def body(tokens, norm_gain, gate_weight, up_weight, down_weight):
    steps, own, half = tokens.shape
    groups, halves = lax.axis_size("gx"), lax.axis_size("gy")
    units = gate_weight.shape[1]
    own_rows = steps * own
    rows = own_rows * groups
    masks = [1 << k for k in range(groups.bit_length() - 1)]
    x = tokens.reshape(own_rows, half)

    pads = (call(empty_kernel, Shape(PAD, f32)),) * PADS
    sums = call(squares_kernel, Shape((own_rows, 128), f32), x, pads=pads)
    held = call(
        functools.partial(norm_kernel, half * halves),
        Shape((own_rows, half), bf16),
        x, sums, swap(sums, "gy", halves, 1), norm_gain.reshape(1, half),
    )
    for mask in reversed(masks):
        held = call(join_kernel, Shape((2 * held.shape[0], half), bf16), held, swap(held, "gx", groups, mask))
    gate = call(project_kernel, Shape((rows, units), f32), held, gate_weight)
    gate_other = swap(gate, "gy", halves, 1)
    up = call(project_kernel, Shape((rows, units), f32), held, up_weight)
    up_other = swap(up, "gy", halves, 1)

    chunk = max(c for c in range(16, 257, 16) if units % c == 0)
    slots = 6
    keep, send = call(
        functools.partial(down_kernel, chunk, slots),
        (Shape((rows // 2, half), f32),) * 2,
        gate, gate_other, up, up_other, down_weight,
        specs=[VMEM] * 4 + [HBM],
        scratch=[
            pltpu.VMEM((rows, half), f32),
            pltpu.VMEM((rows, units), bf16),
            pltpu.VMEM((slots, chunk, half), bf16),
            pltpu.SemaphoreType.DMA((slots,)),
        ],
        limit=42,
    )
    for mask in masks[:-1]:
        part = Shape((keep.shape[0] // 2, half), f32)
        keep, send = call(add_kernel, (part, part), keep, swap(send, "gx", groups, mask))
    out = call(last_kernel, Shape((own_rows, half), bf16), keep, swap(send, "gx", groups, masks[-1]))
    return out.reshape(steps, own, half)


def solution(mesh):
    placed = (P(None, ("grp", "gx"), "gy"), P("gy"), P("gy", "gx"), P("gy", "gx"), P("gx", "gy"))
    return jax.shard_map(
        body, mesh=mesh, in_specs=placed, out_specs=P(None, ("grp", "gx"), "gy"), check_vma=False
    )
```

```python
import functools

import jax
import jax.numpy as jnp
from jax import lax
from jax.experimental import pallas as pl
from jax.experimental.pallas import tpu as pltpu
from jax.sharding import PartitionSpec as P

epsilon = 1e-05
f32, bf16 = jnp.float32, jnp.bfloat16
MiB = 2**20
VMEM = pl.BlockSpec(memory_space=pltpu.VMEM)
HBM = pl.BlockSpec(memory_space=pl.ANY)
Shape = jax.ShapeDtypeStruct

PAD = (512, 1024)
PADS = 48
UP_SHARE, GATE_SHARE = 2, 7


def call(kernel, outs, *args, pads=(), specs=None, scratch=(), limit=2, flops=0):
    skip = len(pads)
    specs = specs or [VMEM] * len(args)
    return pl.pallas_call(
        lambda *refs: kernel(*refs[skip:]),
        out_shape=outs,
        in_specs=[VMEM] * skip + specs,
        out_specs=jax.tree.map(lambda _: VMEM, outs),
        scratch_shapes=scratch,
        cost_estimate=pl.CostEstimate(flops=flops, bytes_accessed=flops // 16, transcendentals=0),
        compiler_params=pltpu.CompilerParams(vmem_limit_bytes=limit * MiB),
    )(*pads, *args)


def empty_kernel(out_ref):
    pass


def squares_kernel(x_ref, sums_ref):
    x = x_ref[...].astype(f32)
    sums_ref[...] = jnp.broadcast_to(jnp.sum(x * x, axis=1, keepdims=True), sums_ref.shape)


def norm_kernel(width, x_ref, own_ref, other_ref, gain_ref, out_ref):
    mean_square = (own_ref[:, :1] + other_ref[:, :1]) / width
    x = x_ref[...].astype(f32)
    out_ref[...] = (x * lax.rsqrt(mean_square + epsilon) * gain_ref[...]).astype(bf16)


def join_kernel(first_ref, second_ref, out_ref):
    rows = first_ref.shape[0]
    out_ref[:rows, :] = first_ref[...]
    out_ref[rows:, :] = second_ref[...]


def project_kernel(ahead, chunk, first, x_ref, w_ref, down_ref, out_ref, *rest):
    copies = []
    if ahead:
        taken_ref, sems = rest
        for k in range(ahead):
            copies.append(
                pltpu.make_async_copy(
                    down_ref.at[pl.ds((first + k) * chunk, chunk), :],
                    taken_ref.at[pl.ds(k * chunk, chunk), :],
                    sems.at[k],
                )
            )
            copies[-1].start()
    columns = w_ref.shape[1]
    for c in range(0, columns, 256):
        e = min(c + 256, columns)
        out_ref[:, c:e] = jnp.dot(x_ref[...], w_ref[:, c:e], preferred_element_type=f32)
    for copy in copies:
        copy.wait()


def down_kernel(chunk, counts, g_ref, g2_ref, u_ref, u2_ref, w_ref, *rest):
    taken, (keep_ref, send_ref, acc_ref, h_ref, buf_ref, sems) = rest[:-6], rest[-6:]
    width = w_ref.shape[1]
    before = sum(counts[:-1])
    copies = []
    for k in range(counts[-1]):
        copies.append(
            pltpu.make_async_copy(w_ref.at[pl.ds((before + k) * chunk, chunk), :], buf_ref.at[k], sems.at[k])
        )
        copies[-1].start()
    v = g_ref[...] + g2_ref[...]
    h_ref[...] = (v / (1.0 + jnp.exp(-v)) * (u_ref[...] + u2_ref[...])).astype(bf16)
    k = 0
    for ref, count in zip((*taken, buf_ref), [n for n in counts if n]):
        for j in range(count):
            if ref is buf_ref:
                copies[j].wait()
                place = (j, slice(None))
            else:
                place = (slice(j * chunk, (j + 1) * chunk),)
            h = h_ref[:, k * chunk : (k + 1) * chunk]
            for c in range(0, width, 512):
                part = jnp.dot(h, ref[(*place, slice(c, c + 512))], preferred_element_type=f32)
                acc_ref[:, c : c + 512] = part if k == 0 else acc_ref[:, c : c + 512] + part
            k += 1
    rows = keep_ref.shape[0]
    keep_ref[...] = acc_ref[:rows, :]
    send_ref[...] = acc_ref[rows:, :].astype(send_ref.dtype)


def add_kernel(a_ref, b_ref, keep_ref, send_ref):
    rows = keep_ref.shape[0]
    total = a_ref[...] + b_ref[...].astype(f32)
    keep_ref[...] = total[:rows]
    send_ref[...] = total[rows:].astype(send_ref.dtype)


def last_kernel(a_ref, b_ref, out_ref):
    out_ref[...] = (a_ref[...] + b_ref[...].astype(f32)).astype(bf16)


def swap(x, axis, size, mask):
    return lax.ppermute(x, axis, [(i, i ^ mask) for i in range(size)])


def body(tokens, norm_gain, gate_weight, up_weight, down_weight):
    steps, own, half = tokens.shape
    groups, halves = lax.axis_size("gx"), lax.axis_size("gy")
    units = gate_weight.shape[1]
    own_rows = steps * own
    rows = own_rows * groups
    masks = [1 << k for k in range(groups.bit_length() - 1)]
    x = tokens.reshape(own_rows, half)

    pads = (call(empty_kernel, Shape(PAD, f32)),) * PADS
    sums = call(squares_kernel, Shape((own_rows, 128), f32), x, pads=pads)
    held = call(
        functools.partial(norm_kernel, half * halves),
        Shape((own_rows, half), bf16),
        x, sums, swap(sums, "gy", halves, 1), norm_gain.reshape(1, half),
    )
    for mask in reversed(masks):
        held = call(join_kernel, Shape((2 * held.shape[0], half), bf16), held, swap(held, "gx", groups, mask))
    chunk = max(c for c in range(16, 257, 16) if units % c == 0)
    count = units // chunk
    counts = (count * UP_SHARE // 13, count * GATE_SHARE // 13)
    counts = (*counts, count - sum(counts))

    def project(weight, first, ahead):
        outs = [Shape((rows, units), f32)]
        scratch = []
        if ahead:
            outs.append(Shape((ahead * chunk, half), bf16))
            scratch.append(pltpu.SemaphoreType.DMA((ahead,)))
        return call(
            functools.partial(project_kernel, ahead, chunk, first),
            outs, held, weight, down_weight,
            specs=[VMEM, VMEM, HBM], scratch=scratch, flops=2 * rows * weight.size,
        )

    up, *taken_up = project(up_weight, 0, counts[0])
    up_other = swap(up, "gy", halves, 1)
    gate, *taken_gate = project(gate_weight, counts[0], counts[1])
    gate_other = swap(gate, "gy", halves, 1)
    taken = (*taken_up, *taken_gate)
    keep, send = call(
        functools.partial(down_kernel, chunk, counts),
        (Shape((rows // 2, half), f32), Shape((rows // 2, half), bf16)),
        gate, gate_other, up, up_other, down_weight, *taken,
        specs=[VMEM] * 4 + [HBM] + [VMEM] * len(taken),
        scratch=[
            pltpu.VMEM((rows, half), f32),
            pltpu.VMEM((rows, units), bf16),
            pltpu.VMEM((counts[-1], chunk, half), bf16),
            pltpu.SemaphoreType.DMA((counts[-1],)),
        ],
        limit=11, flops=2 * rows * down_weight.size,
    )
    for mask in masks[:-1]:
        parts = (Shape((keep.shape[0] // 2, half), f32), Shape((keep.shape[0] // 2, half), bf16))
        keep, send = call(add_kernel, parts, keep, swap(send, "gx", groups, mask))
    out = call(last_kernel, Shape((own_rows, half), bf16), keep, swap(send, "gx", groups, masks[-1]))
    return out.reshape(steps, own, half)


def solution(mesh):
    placed = (P(None, ("grp", "gx"), "gy"), P("gy"), P("gy", "gx"), P("gy", "gx"), P("gx", "gy"))
    return jax.shard_map(
        body, mesh=mesh, in_specs=placed, out_specs=P(None, ("grp", "gx"), "gy"), check_vma=False
    )
```

```python
import functools

import jax
import jax.numpy as jnp
from jax import lax
from jax.experimental import pallas as pl
from jax.experimental.pallas import tpu as pltpu
from jax.sharding import PartitionSpec as P

epsilon = 1e-05
f32, bf16 = jnp.float32, jnp.bfloat16
MiB = 2**20
VMEM = pl.BlockSpec(memory_space=pltpu.VMEM)
HBM = pl.BlockSpec(memory_space=pl.ANY)
Shape = jax.ShapeDtypeStruct

PAD = (512, 1024)
PADS = 48
UP_SHARE, GATE_SHARE = 2, 5
DOWN_LIMIT = 15
LANES = 128


def call(kernel, outs, *args, pads=(), specs=None, scratch=(), limit=0, flops=0):
    skip = len(pads)
    specs = specs or [VMEM] * len(args)
    limit = max(limit, 2, *(a.shape[0] // 8 for a in args if a.shape[0] <= 256))
    return pl.pallas_call(
        lambda *refs: kernel(*refs[skip:]),
        out_shape=outs,
        in_specs=[VMEM] * skip + specs,
        out_specs=jax.tree.map(lambda _: VMEM, outs),
        scratch_shapes=scratch,
        cost_estimate=pl.CostEstimate(flops=flops, bytes_accessed=flops // 16, transcendentals=0),
        compiler_params=pltpu.CompilerParams(vmem_limit_bytes=limit * MiB),
    )(*pads, *args)


def empty_kernel(out_ref):
    pass


def mark_kernel(out_ref):
    out_ref[...] = jnp.zeros_like(out_ref)


def join_kernel(first_ref, second_ref, *rest):
    out_ref = rest[-1]
    rows = first_ref.shape[0]
    out_ref[:rows, :] = first_ref[...]
    out_ref[rows:, :] = second_ref[...]


def prepare_kernel(first_ref, second_ref, gain_ref, high_ref, low_ref, sums_ref):
    rows = first_ref.shape[0]
    for ref, at in ((first_ref, slice(0, rows)), (second_ref, slice(rows, None))):
        x = ref[...].astype(f32)
        sums_ref[at, :] = jnp.broadcast_to(jnp.sum(x * x, axis=1, keepdims=True), (rows, LANES))
        scaled = x * gain_ref[...]
        high = scaled.astype(bf16)
        high_ref[at, :] = high
        low_ref[at, :] = (scaled - high.astype(f32)).astype(bf16)


def project_kernel(ahead, chunk, first, high_ref, low_ref, w_ref, down_ref, sums_ref, *rest):
    out_ref, *rest = rest
    copies = []
    if ahead:
        taken_ref, sem = rest
        copies.append(pltpu.make_async_copy(down_ref.at[pl.ds(first * chunk, ahead * chunk), :], taken_ref, sem))
        copies[-1].start()
    x = jnp.concatenate([high_ref[...], low_ref[...]], axis=0)
    rows = high_ref.shape[0]
    out_ref[:, :LANES] = sums_ref[...]
    columns = w_ref.shape[1]
    for c in range(0, columns, 256):
        e = min(c + 256, columns)
        both = jnp.dot(x, w_ref[:, c:e], preferred_element_type=f32)
        out_ref[:, LANES + c : LANES + e] = both[:rows] + both[rows:]
    for copy in copies:
        copy.wait()


def down_kernel(chunk, counts, features, g_ref, g2_ref, u_ref, u2_ref, w_ref, *rest):
    taken, (keep_ref, send_ref, acc_ref, h_ref, buf_ref, sem) = rest[:-6], rest[-6:]
    width = w_ref.shape[1]
    tail = pltpu.make_async_copy(
        w_ref.at[pl.ds(sum(counts[:-1]) * chunk, counts[-1] * chunk), :], buf_ref, sem
    )
    tail.start()
    scale = lax.rsqrt((u_ref[:, :1] + u2_ref[:, :1]) / features + epsilon)
    v = (g_ref[:, LANES:] + g2_ref[:, LANES:]) * scale
    h_ref[...] = (v / (1.0 + jnp.exp(-v)) * ((u_ref[:, LANES:] + u2_ref[:, LANES:]) * scale)).astype(bf16)
    rows = keep_ref.shape[0]
    place = 0
    for c in range(0, width, 512) if taken else ():
        place = 0
        total = None
        for ref in taken:
            part = jnp.dot(
                h_ref[:, place : place + ref.shape[0]], ref[:, c : c + 512], preferred_element_type=f32
            )
            total = part if total is None else total + part
            place += ref.shape[0]
        acc_ref[:, c : c + 512] = total
    tail.wait()
    for c in range(0, width, 512):
        total = jnp.dot(h_ref[:, place:], buf_ref[:, c : c + 512], preferred_element_type=f32)
        if taken:
            total = acc_ref[:, c : c + 512] + total
        keep_ref[:, c : c + 512] = total[:rows]
        send_ref[:, c : c + 512] = total[rows:].astype(send_ref.dtype)


def add_kernel(a_ref, b_ref, keep_ref, send_ref):
    rows = keep_ref.shape[0]
    total = a_ref[...] + b_ref[...].astype(f32)
    keep_ref[...] = total[:rows]
    send_ref[...] = total[rows:].astype(send_ref.dtype)


def last_kernel(a_ref, b_ref, out_ref):
    out_ref[...] = (a_ref[...] + b_ref[...].astype(f32)).astype(bf16)


def swap(x, axis, size, mask):
    return lax.ppermute(x, axis, [(i, i ^ mask) for i in range(size)])


def body(tokens, norm_gain, gate_weight, up_weight, down_weight):
    steps, own, half = tokens.shape
    groups, halves = lax.axis_size("gx"), lax.axis_size("gy")
    units = gate_weight.shape[1]
    own_rows = steps * own
    rows = own_rows * groups
    masks = [1 << k for k in range(groups.bit_length() - 1)]
    x = tokens.reshape(own_rows, half)

    pads = (call(empty_kernel, Shape(PAD, f32)),) * PADS
    mark = call(mark_kernel, Shape((8, LANES), f32), pads=pads)
    held, mark = lax.optimization_barrier((x, mark))
    for mask in reversed(masks[1:]):
        held = call(
            join_kernel, Shape((2 * held.shape[0], half), bf16), held, swap(held, "gx", groups, mask), mark
        )
    part = Shape((rows, half), bf16)
    high, low, sums = call(
        prepare_kernel,
        (part, part, Shape((rows, LANES), f32)),
        held, swap(held, "gx", groups, masks[0]), norm_gain.reshape(1, half),
    )
    chunk = max(c for c in range(16, 257, 16) if units % c == 0)
    count = units // chunk
    counts = (count * UP_SHARE // 13, count * GATE_SHARE // 13)
    counts = (*counts, count - sum(counts))

    def project(weight, first, ahead):
        outs = [Shape((rows, LANES + units), f32)]
        scratch = []
        if ahead:
            outs.append(Shape((ahead * chunk, half), bf16))
            scratch.append(pltpu.SemaphoreType.DMA)
        return call(
            functools.partial(project_kernel, ahead, chunk, first),
            outs, high, low, weight, down_weight, sums,
            specs=[VMEM] * 3 + [HBM, VMEM], scratch=scratch, flops=2 * rows * weight.size,
        )

    up, *taken_up = project(up_weight, 0, counts[0])
    up_other = swap(up, "gy", halves, 1)
    gate, *taken_gate = project(gate_weight, counts[0], counts[1])
    gate_other = swap(gate, "gy", halves, 1)
    taken = (*taken_up, *taken_gate)
    keep, send = call(
        functools.partial(down_kernel, chunk, counts, half * halves),
        (Shape((rows // 2, half), f32), Shape((rows // 2, half), bf16)),
        gate, gate_other, up, up_other, down_weight, *taken,
        specs=[VMEM] * 4 + [HBM] + [VMEM] * len(taken),
        scratch=[
            pltpu.VMEM((rows, half), f32),
            pltpu.VMEM((rows, units), bf16),
            pltpu.VMEM((counts[-1] * chunk, half), bf16),
            pltpu.SemaphoreType.DMA,
        ],
        limit=DOWN_LIMIT, flops=2 * rows * down_weight.size,
    )
    for mask in masks[:-1]:
        parts = (Shape((keep.shape[0] // 2, half), f32), Shape((keep.shape[0] // 2, half), bf16))
        keep, send = call(add_kernel, parts, keep, swap(send, "gx", groups, mask))
    out = call(last_kernel, Shape((own_rows, half), bf16), keep, swap(send, "gx", groups, masks[-1]))
    return out.reshape(steps, own, half)


def solution(mesh):
    placed = (P(None, ("grp", "gx"), "gy"), P("gy"), P("gy", "gx"), P("gy", "gx"), P("gx", "gy"))
    return jax.shard_map(
        body, mesh=mesh, in_specs=placed, out_specs=P(None, ("grp", "gx"), "gy"), check_vma=False
    )
```

```python
import functools

import jax
import jax.numpy as jnp
from jax import lax
from jax.experimental import pallas as pl
from jax.experimental.pallas import tpu as pltpu
from jax.sharding import PartitionSpec as P

epsilon = 1e-05
f32, bf16 = jnp.float32, jnp.bfloat16
MiB = 2**20
VMEM = pl.BlockSpec(memory_space=pltpu.VMEM)
HBM = pl.BlockSpec(memory_space=pl.ANY)
Shape = jax.ShapeDtypeStruct

PAD = (512, 1024)
PADS = 48
UP_SHARE, GATE_SHARE = 2, 5
DOWN_LIMIT = 15


def call(kernel, outs, *args, pads=(), specs=None, scratch=(), limit=0, flops=0):
    skip = len(pads)
    specs = specs or [VMEM] * len(args)
    limit = max(limit, 2, *(a.shape[0] // 8 for a in args if a.shape[0] <= 256))
    return pl.pallas_call(
        lambda *refs: kernel(*refs[skip:]),
        out_shape=outs,
        in_specs=[VMEM] * skip + specs,
        out_specs=jax.tree.map(lambda _: VMEM, outs),
        scratch_shapes=scratch,
        cost_estimate=pl.CostEstimate(flops=flops, bytes_accessed=flops // 16, transcendentals=0),
        compiler_params=pltpu.CompilerParams(vmem_limit_bytes=limit * MiB),
    )(*pads, *args)


def empty_kernel(out_ref):
    pass


def mark_kernel(out_ref):
    out_ref[...] = jnp.zeros_like(out_ref)


def pack_kernel(mark_ref, x_ref, gain_ref, out_ref):
    rows = x_ref.shape[0]
    out_ref[:rows, :] = x_ref[...].astype(f32)
    out_ref[rows:, :] = gain_ref[...]


def norm_kernel(own_ref, other_ref, own_out_ref, other_out_ref):
    rows = own_out_ref.shape[0]
    halves = [ref[:rows, :] for ref in (own_ref, other_ref)]
    features = 2 * own_ref.shape[1]
    mean_square = sum(jnp.sum(x * x, axis=1, keepdims=True) for x in halves) / features
    scale = lax.rsqrt(mean_square + epsilon)
    for x, ref, out_ref in zip(halves, (own_ref, other_ref), (own_out_ref, other_out_ref)):
        out_ref[...] = (x * scale * ref[rows:, :]).astype(bf16)


def join_kernel(first_ref, second_ref, out_ref):
    rows = first_ref.shape[0]
    out_ref[:rows, :] = first_ref[...]
    out_ref[rows:, :] = second_ref[...]


def project_kernel(ahead, chunk, first, x_ref, w_ref, down_ref, out_ref, *rest):
    copies = []
    if ahead:
        taken_ref, sem = rest
        copies.append(pltpu.make_async_copy(down_ref.at[pl.ds(first * chunk, ahead * chunk), :], taken_ref, sem))
        copies[-1].start()
    columns = w_ref.shape[1]
    for c in range(0, columns, 256):
        e = min(c + 256, columns)
        out_ref[:, c:e] = jnp.dot(x_ref[...], w_ref[:, c:e], preferred_element_type=f32)
    for copy in copies:
        copy.wait()


def down_kernel(bounds, g_ref, g2_ref, u_ref, u2_ref, w_ref, *rest):
    taken, (keep_ref, send_ref, acc_ref, h_ref, buf_ref, sems) = rest[:-6], rest[-6:]
    width = w_ref.shape[1]
    start = bounds[0]
    copies = [
        pltpu.make_async_copy(w_ref.at[pl.ds(a, b - a), :], buf_ref.at[pl.ds(a - start, b - a), :], sems.at[k])
        for k, (a, b) in enumerate(zip(bounds, bounds[1:]))
    ]
    for copy in copies:
        copy.start()
    v = g_ref[...] + g2_ref[...]
    h_ref[...] = (v / (1.0 + jnp.exp(-v)) * (u_ref[...] + u2_ref[...])).astype(bf16)
    rows = keep_ref.shape[0]
    passes = [(copy, [(buf_ref, a - start, a, b)]) for copy, a, b in zip(copies, bounds, bounds[1:])]
    if taken:
        place, parts = 0, []
        for ref in taken:
            parts.append((ref, 0, place, place + ref.shape[0]))
            place += ref.shape[0]
        passes.insert(0, (None, parts))
    for k, (copy, parts) in enumerate(passes):
        if copy is not None:
            copy.wait()
        for c in range(0, width, 512):
            total = acc_ref[:, c : c + 512] if k else None
            for ref, at, a, b in parts:
                part = jnp.dot(h_ref[:, a:b], ref[at : at + b - a, c : c + 512], preferred_element_type=f32)
                total = part if total is None else total + part
            if k < len(passes) - 1:
                acc_ref[:, c : c + 512] = total
            else:
                keep_ref[:, c : c + 512] = total[:rows]
                send_ref[:, c : c + 512] = total[rows:].astype(send_ref.dtype)


def add_kernel(a_ref, b_ref, keep_ref, send_ref):
    rows = keep_ref.shape[0]
    total = a_ref[...] + b_ref[...].astype(f32)
    keep_ref[...] = total[:rows]
    send_ref[...] = total[rows:].astype(send_ref.dtype)


def last_kernel(a_ref, b_ref, out_ref):
    out_ref[...] = (a_ref[...] + b_ref[...].astype(f32)).astype(bf16)


def cross(x, groups, mask):
    return lax.ppermute(
        x, ("gx", "gy"), [(2 * i + c, 2 * (i ^ mask) + 1 - c) for i in range(groups) for c in range(2)]
    )


def swap(x, axis, size, mask):
    return lax.ppermute(x, axis, [(i, i ^ mask) for i in range(size)])


def body(tokens, norm_gain, gate_weight, up_weight, down_weight):
    steps, local, half = tokens.shape
    groups, halves = lax.axis_size("gx"), lax.axis_size("gy")
    units = gate_weight.shape[1]
    own_rows = steps * local
    rows = own_rows * groups
    masks = [1 << k for k in range(groups.bit_length() - 1)]
    x = tokens.reshape(own_rows, half)

    pads = (call(empty_kernel, Shape(PAD, f32)),) * PADS
    mark = call(mark_kernel, Shape((8, 128), f32), pads=pads)
    packed = call(pack_kernel, Shape((own_rows + 1, half), f32), mark, x, norm_gain.reshape(1, half))
    own, other = call(
        norm_kernel, (Shape((own_rows, half), bf16),) * 2, packed, swap(packed, "gy", halves, 1)
    )
    held = call(join_kernel, Shape((2 * own_rows, half), bf16), own, cross(other, groups, masks[-1]))
    for mask in reversed(masks[:-1]):
        held = call(join_kernel, Shape((2 * held.shape[0], half), bf16), held, swap(held, "gx", groups, mask))
    chunk = max(c for c in range(16, 257, 16) if units % c == 0)
    count = units // chunk
    counts = (count * UP_SHARE // 13, count * GATE_SHARE // 13)
    counts = (*counts, count - sum(counts))

    def project(weight, first, ahead):
        outs = [Shape((rows, units), f32)]
        scratch = []
        if ahead:
            outs.append(Shape((ahead * chunk, half), bf16))
            scratch.append(pltpu.SemaphoreType.DMA)
        return call(
            functools.partial(project_kernel, ahead, chunk, first),
            outs, held, weight, down_weight,
            specs=[VMEM, VMEM, HBM], scratch=scratch, flops=2 * rows * weight.size,
        )

    up, *taken_up = project(up_weight, 0, counts[0])
    up_other = swap(up, "gy", halves, 1)
    gate, *taken_gate = project(gate_weight, counts[0], counts[1])
    gate_other = swap(gate, "gy", halves, 1)
    taken = (*taken_up, *taken_gate)
    start = sum(counts[:-1]) * chunk
    bounds = (*range(start, units, 2 * chunk), units)
    keep, send = call(
        functools.partial(down_kernel, bounds),
        (Shape((rows // 2, half), f32), Shape((rows // 2, half), bf16)),
        gate, gate_other, up, up_other, down_weight, *taken,
        specs=[VMEM] * 4 + [HBM] + [VMEM] * len(taken),
        scratch=[
            pltpu.VMEM((rows, half), f32),
            pltpu.VMEM((rows, units), bf16),
            pltpu.VMEM((units - start, half), bf16),
            pltpu.SemaphoreType.DMA((len(bounds) - 1,)),
        ],
        limit=DOWN_LIMIT, flops=2 * rows * down_weight.size,
    )
    for mask in masks[:-1]:
        parts = (Shape((keep.shape[0] // 2, half), f32), Shape((keep.shape[0] // 2, half), bf16))
        keep, send = call(add_kernel, parts, keep, swap(send, "gx", groups, mask))
    out = call(last_kernel, Shape((own_rows, half), bf16), keep, swap(send, "gx", groups, masks[-1]))
    return out.reshape(steps, local, half)


def solution(mesh):
    placed = (P(None, ("grp", "gx"), "gy"), P("gy"), P("gy", "gx"), P("gy", "gx"), P("gx", "gy"))
    return jax.shard_map(
        body, mesh=mesh, in_specs=placed, out_specs=P(None, ("grp", "gx"), "gy"), check_vma=False
    )
```

```python
import functools

import jax
import jax.numpy as jnp
from jax import lax
from jax.experimental import pallas as pl
from jax.experimental.pallas import tpu as pltpu
from jax.sharding import PartitionSpec as P

epsilon = 1e-05
f32, bf16 = jnp.float32, jnp.bfloat16
MiB = 2**20
VMEM = pl.BlockSpec(memory_space=pltpu.VMEM)
HBM = pl.BlockSpec(memory_space=pl.ANY)
Shape = jax.ShapeDtypeStruct

PAD = (512, 1024)
PADS = 96
UP_SHARE, GATE_SHARE = 2, 5
DOWN_LIMIT = 15


def call(kernel, outs, *args, pads=(), specs=None, scratch=(), limit=0, flops=0):
    skip = len(pads)
    specs = specs or [VMEM] * len(args)
    limit = max(limit, 2, *(a.shape[0] // 8 for a in args if a.shape[0] <= 256))
    return pl.pallas_call(
        lambda *refs: kernel(*refs[skip:]),
        out_shape=outs,
        in_specs=[VMEM] * skip + specs,
        out_specs=jax.tree.map(lambda _: VMEM, outs),
        scratch_shapes=scratch,
        cost_estimate=pl.CostEstimate(flops=flops, bytes_accessed=flops // 16, transcendentals=0),
        compiler_params=pltpu.CompilerParams(vmem_limit_bytes=limit * MiB),
    )(*pads, *args)


def empty_kernel(out_ref):
    pass


def mark_kernel(out_ref):
    out_ref[...] = jnp.zeros_like(out_ref)


def pack_kernel(mark_ref, x_ref, gain_ref, out_ref):
    rows = x_ref.shape[0]
    out_ref[:rows, :] = x_ref[...].astype(f32)
    out_ref[rows:, :] = gain_ref[...]


def norm_kernel(own_ref, other_ref, own_out_ref, other_out_ref):
    rows = own_out_ref.shape[0]
    halves = [ref[:rows, :] for ref in (own_ref, other_ref)]
    features = 2 * own_ref.shape[1]
    mean_square = sum(jnp.sum(x * x, axis=1, keepdims=True) for x in halves) / features
    scale = lax.rsqrt(mean_square + epsilon)
    for x, ref, out_ref in zip(halves, (own_ref, other_ref), (own_out_ref, other_out_ref)):
        out_ref[...] = (x * scale * ref[rows:, :]).astype(bf16)


def join_kernel(first_ref, second_ref, out_ref):
    rows = first_ref.shape[0]
    out_ref[:rows, :] = first_ref[...]
    out_ref[rows:, :] = second_ref[...]


def project_kernel(ahead, chunk, first, x_ref, w_ref, down_ref, out_ref, *rest):
    copies = []
    if ahead:
        taken_ref, sem = rest
        copies.append(pltpu.make_async_copy(down_ref.at[pl.ds(first * chunk, ahead * chunk), :], taken_ref, sem))
        copies[-1].start()
    columns = w_ref.shape[1]
    for c in range(0, columns, 256):
        e = min(c + 256, columns)
        out_ref[:, c:e] = jnp.dot(x_ref[...], w_ref[:, c:e], preferred_element_type=f32)
    for copy in copies:
        copy.wait()


def down_kernel(bounds, g_ref, g2_ref, u_ref, u2_ref, w_ref, *rest):
    taken, (keep_ref, send_ref, acc_ref, h_ref, buf_ref, sems) = rest[:-6], rest[-6:]
    width = w_ref.shape[1]
    start = bounds[0]
    copies = [
        pltpu.make_async_copy(w_ref.at[pl.ds(a, b - a), :], buf_ref.at[pl.ds(a - start, b - a), :], sems.at[k])
        for k, (a, b) in enumerate(zip(bounds, bounds[1:]))
    ]
    for copy in copies:
        copy.start()
    v = g_ref[...] + g2_ref[...]
    h_ref[...] = (v / (1.0 + jnp.exp(-v)) * (u_ref[...] + u2_ref[...])).astype(bf16)
    rows = keep_ref.shape[0]
    passes = [(copy, [(buf_ref, a - start, a, b)]) for copy, a, b in zip(copies, bounds, bounds[1:])]
    if taken:
        place, parts = 0, []
        for ref in taken:
            parts.append((ref, 0, place, place + ref.shape[0]))
            place += ref.shape[0]
        passes.insert(0, (None, parts))
    for k, (copy, parts) in enumerate(passes):
        if copy is not None:
            copy.wait()
        for c in range(0, width, 512):
            total = acc_ref[:, c : c + 512] if k else None
            for ref, at, a, b in parts:
                part = jnp.dot(h_ref[:, a:b], ref[at : at + b - a, c : c + 512], preferred_element_type=f32)
                total = part if total is None else total + part
            if k < len(passes) - 1:
                acc_ref[:, c : c + 512] = total
            else:
                keep_ref[:, c : c + 512] = total[:rows]
                send_ref[:, c : c + 512] = total[rows:].astype(send_ref.dtype)


def add_kernel(a_ref, b_ref, keep_ref, send_ref):
    rows = keep_ref.shape[0]
    total = a_ref[...] + b_ref[...].astype(f32)
    keep_ref[...] = total[:rows]
    send_ref[...] = total[rows:].astype(send_ref.dtype)


def last_kernel(a_ref, b_ref, out_ref):
    out_ref[...] = (a_ref[...] + b_ref[...].astype(f32)).astype(bf16)


def cross(x, groups, mask):
    return lax.ppermute(
        x, ("gx", "gy"), [(2 * i + c, 2 * (i ^ mask) + 1 - c) for i in range(groups) for c in range(2)]
    )


def swap(x, axis, size, mask):
    return lax.ppermute(x, axis, [(i, i ^ mask) for i in range(size)])


def body(tokens, norm_gain, gate_weight, up_weight, down_weight):
    steps, local, half = tokens.shape
    groups, halves = lax.axis_size("gx"), lax.axis_size("gy")
    units = gate_weight.shape[1]
    own_rows = steps * local
    rows = own_rows * groups
    masks = [1 << k for k in range(groups.bit_length() - 1)]
    x = tokens.reshape(own_rows, half)

    pads = (call(empty_kernel, Shape(PAD, f32)),) * PADS
    mark = call(mark_kernel, Shape((8, 128), f32), pads=pads)
    packed = call(pack_kernel, Shape((own_rows + 1, half), f32), mark, x, norm_gain.reshape(1, half))
    own, other = call(
        norm_kernel, (Shape((own_rows, half), bf16),) * 2, packed, swap(packed, "gy", halves, 1)
    )
    held = call(join_kernel, Shape((2 * own_rows, half), bf16), own, cross(other, groups, masks[-1]))
    for mask in reversed(masks[:-1]):
        held = call(join_kernel, Shape((2 * held.shape[0], half), bf16), held, swap(held, "gx", groups, mask))
    down_weight = pltpu.with_memory_space_constraint(down_weight, pltpu.HBM)
    chunk = max(c for c in range(16, 257, 16) if units % c == 0)
    count = units // chunk
    counts = (count * UP_SHARE // 13, count * GATE_SHARE // 13)
    counts = (*counts, count - sum(counts))

    def project(weight, first, ahead):
        outs = [Shape((rows, units), f32)]
        scratch = []
        if ahead:
            outs.append(Shape((ahead * chunk, half), bf16))
            scratch.append(pltpu.SemaphoreType.DMA)
        return call(
            functools.partial(project_kernel, ahead, chunk, first),
            outs, held, weight, down_weight,
            specs=[VMEM, VMEM, HBM], scratch=scratch, flops=2 * rows * weight.size,
        )

    up, *taken_up = project(up_weight, 0, counts[0])
    up_other = swap(up, "gy", halves, 1)
    gate, *taken_gate = project(gate_weight, counts[0], counts[1])
    gate_other = swap(gate, "gy", halves, 1)
    taken = (*taken_up, *taken_gate)
    start = sum(counts[:-1]) * chunk
    bounds = (*range(start, units, 2 * chunk), units)
    keep, send = call(
        functools.partial(down_kernel, bounds),
        (Shape((rows // 2, half), f32), Shape((rows // 2, half), bf16)),
        gate, gate_other, up, up_other, down_weight, *taken,
        specs=[VMEM] * 4 + [HBM] + [VMEM] * len(taken),
        scratch=[
            pltpu.VMEM((rows, half), f32),
            pltpu.VMEM((rows, units), bf16),
            pltpu.VMEM((units - start, half), bf16),
            pltpu.SemaphoreType.DMA((len(bounds) - 1,)),
        ],
        limit=DOWN_LIMIT, flops=2 * rows * down_weight.size,
    )
    for mask in masks[:-1]:
        parts = (Shape((keep.shape[0] // 2, half), f32), Shape((keep.shape[0] // 2, half), bf16))
        keep, send = call(add_kernel, parts, keep, swap(send, "gx", groups, mask))
    out = call(last_kernel, Shape((own_rows, half), bf16), keep, swap(send, "gx", groups, masks[-1]))
    return out.reshape(steps, local, half)


def solution(mesh):
    placed = (P(None, ("grp", "gx"), "gy"), P("gy"), P("gy", "gx"), P("gy", "gx"), P("gx", "gy"))
    return jax.shard_map(
        body, mesh=mesh, in_specs=placed, out_specs=P(None, ("grp", "gx"), "gy"), check_vma=False
    )
```

```python
import functools

import jax
import jax.numpy as jnp
from jax import lax
from jax.experimental import pallas as pl
from jax.experimental.pallas import tpu as pltpu
from jax.sharding import PartitionSpec as P

epsilon = 1e-05
f32, bf16 = jnp.float32, jnp.bfloat16
MiB = 2**20
VMEM = pl.BlockSpec(memory_space=pltpu.VMEM)
HBM = pl.BlockSpec(memory_space=pl.ANY)
Shape = jax.ShapeDtypeStruct

PAD = (512, 1024)
PADS = 96
UP_SHARE, GATE_SHARE = 2, 5
DOWN_LIMIT = 15


def call(kernel, outs, *args, pads=(), specs=None, scratch=(), limit=0, flops=0):
    skip = len(pads)
    specs = specs or [VMEM] * len(args)
    limit = max(limit, 2, *(a.shape[0] // 8 for a in args if a.shape[0] <= 256))
    return pl.pallas_call(
        lambda *refs: kernel(*refs[skip:]),
        out_shape=outs,
        in_specs=[VMEM] * skip + specs,
        out_specs=jax.tree.map(lambda _: VMEM, outs),
        scratch_shapes=scratch,
        cost_estimate=pl.CostEstimate(flops=flops, bytes_accessed=flops // 16, transcendentals=0),
        compiler_params=pltpu.CompilerParams(vmem_limit_bytes=limit * MiB),
    )(*pads, *args)


def empty_kernel(out_ref):
    pass


def mark_kernel(out_ref):
    out_ref[...] = jnp.zeros_like(out_ref)


def pack_kernel(mark_ref, x_ref, gain_ref, out_ref):
    rows = x_ref.shape[0]
    out_ref[:rows, :] = x_ref[...].astype(f32)
    out_ref[rows:, :] = gain_ref[...]


def norm_kernel(own_ref, other_ref, own_out_ref, other_out_ref):
    rows = own_out_ref.shape[0]
    halves = [ref[:rows, :] for ref in (own_ref, other_ref)]
    features = 2 * own_ref.shape[1]
    mean_square = sum(jnp.sum(x * x, axis=1, keepdims=True) for x in halves) / features
    scale = lax.rsqrt(mean_square + epsilon)
    for x, ref, out_ref in zip(halves, (own_ref, other_ref), (own_out_ref, other_out_ref)):
        out_ref[...] = (x * scale * ref[rows:, :]).astype(bf16)


def join_kernel(first_ref, second_ref, out_ref):
    rows = first_ref.shape[0]
    out_ref[:rows, :] = first_ref[...]
    out_ref[rows:, :] = second_ref[...]


def project_kernel(ahead, chunk, first, x_ref, w_ref, down_ref, out_ref, send_ref, *rest):
    copies = []
    if ahead:
        taken_ref, sem = rest
        copies.append(pltpu.make_async_copy(down_ref.at[pl.ds(first * chunk, ahead * chunk), :], taken_ref, sem))
        copies[-1].start()
    columns = w_ref.shape[1]
    for c in range(0, columns, 256):
        e = min(c + 256, columns)
        part = jnp.dot(x_ref[...], w_ref[:, c:e], preferred_element_type=f32)
        out_ref[:, c:e] = part
        send_ref[:, c:e] = part.astype(send_ref.dtype)
    for copy in copies:
        copy.wait()


def down_kernel(bounds, g_ref, g2_ref, u_ref, u2_ref, w_ref, *rest):
    taken, (keep_ref, send_ref, acc_ref, h_ref, buf_ref, sems) = rest[:-6], rest[-6:]
    width = w_ref.shape[1]
    start = bounds[0]
    copies = [
        pltpu.make_async_copy(w_ref.at[pl.ds(a, b - a), :], buf_ref.at[pl.ds(a - start, b - a), :], sems.at[k])
        for k, (a, b) in enumerate(zip(bounds, bounds[1:]))
    ]
    for copy in copies:
        copy.start()
    v = g_ref[...] + g2_ref[...].astype(f32)
    h_ref[...] = (v / (1.0 + jnp.exp(-v)) * (u_ref[...] + u2_ref[...].astype(f32))).astype(bf16)
    rows = keep_ref.shape[0]
    passes = [(copy, [(buf_ref, a - start, a, b)]) for copy, a, b in zip(copies, bounds, bounds[1:])]
    if taken:
        place, parts = 0, []
        for ref in taken:
            parts.append((ref, 0, place, place + ref.shape[0]))
            place += ref.shape[0]
        passes.insert(0, (None, parts))
    for k, (copy, parts) in enumerate(passes):
        if copy is not None:
            copy.wait()
        for c in range(0, width, 512):
            total = acc_ref[:, c : c + 512] if k else None
            for ref, at, a, b in parts:
                part = jnp.dot(h_ref[:, a:b], ref[at : at + b - a, c : c + 512], preferred_element_type=f32)
                total = part if total is None else total + part
            if k < len(passes) - 1:
                acc_ref[:, c : c + 512] = total
            else:
                keep_ref[:, c : c + 512] = total[:rows]
                send_ref[:, c : c + 512] = total[rows:].astype(send_ref.dtype)


def add_kernel(a_ref, b_ref, keep_ref, send_ref):
    rows = keep_ref.shape[0]
    total = a_ref[...] + b_ref[...].astype(f32)
    keep_ref[...] = total[:rows]
    send_ref[...] = total[rows:].astype(send_ref.dtype)


def last_kernel(a_ref, b_ref, out_ref):
    out_ref[...] = (a_ref[...] + b_ref[...].astype(f32)).astype(bf16)


def cross(x, groups, mask):
    return lax.ppermute(
        x, ("gx", "gy"), [(2 * i + c, 2 * (i ^ mask) + 1 - c) for i in range(groups) for c in range(2)]
    )


def swap(x, axis, size, mask):
    return lax.ppermute(x, axis, [(i, i ^ mask) for i in range(size)])


def body(tokens, norm_gain, gate_weight, up_weight, down_weight):
    steps, local, half = tokens.shape
    groups, halves = lax.axis_size("gx"), lax.axis_size("gy")
    units = gate_weight.shape[1]
    own_rows = steps * local
    rows = own_rows * groups
    masks = [1 << k for k in range(groups.bit_length() - 1)]
    x = tokens.reshape(own_rows, half)

    pads = (call(empty_kernel, Shape(PAD, f32)),) * PADS
    mark = call(mark_kernel, Shape((8, 128), f32), pads=pads)
    packed = call(pack_kernel, Shape((own_rows + 1, half), f32), mark, x, norm_gain.reshape(1, half))
    own, other = call(
        norm_kernel, (Shape((own_rows, half), bf16),) * 2, packed, swap(packed, "gy", halves, 1)
    )
    held = call(join_kernel, Shape((2 * own_rows, half), bf16), own, cross(other, groups, masks[-1]))
    for mask in reversed(masks[:-1]):
        held = call(join_kernel, Shape((2 * held.shape[0], half), bf16), held, swap(held, "gx", groups, mask))
    down_weight = pltpu.with_memory_space_constraint(down_weight, pltpu.HBM)
    chunk = max(c for c in range(16, 257, 16) if units % c == 0)
    count = units // chunk
    counts = (count * UP_SHARE // 13, count * GATE_SHARE // 13)
    counts = (*counts, count - sum(counts))

    def project(weight, first, ahead):
        outs = [Shape((rows, units), f32), Shape((rows, units), bf16)]
        scratch = []
        if ahead:
            outs.append(Shape((ahead * chunk, half), bf16))
            scratch.append(pltpu.SemaphoreType.DMA)
        return call(
            functools.partial(project_kernel, ahead, chunk, first),
            outs, held, weight, down_weight,
            specs=[VMEM, VMEM, HBM], scratch=scratch, flops=2 * rows * weight.size,
        )

    up, up_send, *taken_up = project(up_weight, 0, counts[0])
    up_other = swap(up_send, "gy", halves, 1)
    gate, gate_send, *taken_gate = project(gate_weight, counts[0], counts[1])
    gate_other = swap(gate_send, "gy", halves, 1)
    taken = (*taken_up, *taken_gate)
    start = sum(counts[:-1]) * chunk
    bounds = [start]
    while bounds[-1] < units:
        bounds.append(bounds[-1] + (2 * chunk if units - bounds[-1] > 3 * chunk else chunk))
    keep, send = call(
        functools.partial(down_kernel, bounds),
        (Shape((rows // 2, half), f32), Shape((rows // 2, half), bf16)),
        gate, gate_other, up, up_other, down_weight, *taken,
        specs=[VMEM] * 4 + [HBM] + [VMEM] * len(taken),
        scratch=[
            pltpu.VMEM((rows, half), f32),
            pltpu.VMEM((rows, units), bf16),
            pltpu.VMEM((units - start, half), bf16),
            pltpu.SemaphoreType.DMA((len(bounds) - 1,)),
        ],
        limit=DOWN_LIMIT, flops=2 * rows * down_weight.size,
    )
    for mask in masks[:-1]:
        parts = (Shape((keep.shape[0] // 2, half), f32), Shape((keep.shape[0] // 2, half), bf16))
        keep, send = call(add_kernel, parts, keep, swap(send, "gx", groups, mask))
    out = call(last_kernel, Shape((own_rows, half), bf16), keep, swap(send, "gx", groups, masks[-1]))
    return out.reshape(steps, local, half)


def solution(mesh):
    placed = (P(None, ("grp", "gx"), "gy"), P("gy"), P("gy", "gx"), P("gy", "gx"), P("gx", "gy"))
    return jax.shard_map(
        body, mesh=mesh, in_specs=placed, out_specs=P(None, ("grp", "gx"), "gy"), check_vma=False
    )
```

```python
import functools

import jax
import jax.numpy as jnp
from jax import lax
from jax.experimental import pallas as pl
from jax.experimental.pallas import tpu as pltpu
from jax.sharding import PartitionSpec as P

epsilon = 1e-05
f32, bf16 = jnp.float32, jnp.bfloat16
MiB = 2**20
VMEM = pl.BlockSpec(memory_space=pltpu.VMEM)
HBM = pl.BlockSpec(memory_space=pl.ANY)
Shape = jax.ShapeDtypeStruct

PAD = (512, 1024)
PADS = 96
UP_SHARE, GATE_SHARE = 2, 5
DOWN_LIMIT = 15


def call(kernel, outs, *args, pads=(), specs=None, scratch=(), limit=0, flops=0):
    skip = len(pads)
    specs = specs or [VMEM] * len(args)
    limit = max(limit, 2, *(a.shape[0] // 8 for a in args if a.shape[0] <= 256))
    return pl.pallas_call(
        lambda *refs: kernel(*refs[skip:]),
        out_shape=outs,
        in_specs=[VMEM] * skip + specs,
        out_specs=jax.tree.map(lambda _: VMEM, outs),
        scratch_shapes=scratch,
        cost_estimate=pl.CostEstimate(flops=flops, bytes_accessed=flops // 16, transcendentals=0),
        compiler_params=pltpu.CompilerParams(vmem_limit_bytes=limit * MiB),
    )(*pads, *args)


def empty_kernel(out_ref):
    pass


def mark_kernel(out_ref):
    out_ref[...] = jnp.zeros_like(out_ref)


def pack_kernel(mark_ref, x_ref, gain_ref, out_ref):
    rows = x_ref.shape[0]
    out_ref[:rows, :] = x_ref[...].astype(f32)
    out_ref[rows:, :] = gain_ref[...]


def norm_kernel(own_ref, other_ref, own_out_ref, other_out_ref):
    rows = own_out_ref.shape[0]
    halves = [ref[:rows, :] for ref in (own_ref, other_ref)]
    features = 2 * own_ref.shape[1]
    mean_square = sum(jnp.sum(x * x, axis=1, keepdims=True) for x in halves) / features
    scale = lax.rsqrt(mean_square + epsilon)
    for x, ref, out_ref in zip(halves, (own_ref, other_ref), (own_out_ref, other_out_ref)):
        out_ref[...] = (x * scale * ref[rows:, :]).astype(bf16)


def join_kernel(first_ref, second_ref, out_ref):
    rows = first_ref.shape[0]
    out_ref[:rows, :] = first_ref[...]
    out_ref[rows:, :] = second_ref[...]


def project_kernel(narrow, ahead, chunk, first, x_ref, w_ref, down_ref, out_ref, *rest):
    copies = []
    send_ref = None if narrow is None else rest[0]
    if ahead:
        taken_ref, sem = rest[-2:]
        copies.append(pltpu.make_async_copy(down_ref.at[pl.ds(first * chunk, ahead * chunk), :], taken_ref, sem))
        copies[-1].start()
    columns = w_ref.shape[1]
    for c in range(0, columns, 256):
        e = min(c + 256, columns)
        part = jnp.dot(x_ref[...], w_ref[:, c:e], preferred_element_type=f32)
        out_ref[:, c:e] = part
        if send_ref is not None:
            send_ref[:, c:e] = part.astype(narrow)
    for copy in copies:
        copy.wait()


def down_kernel(bounds, g_ref, g2_ref, u_ref, u2_ref, w_ref, *rest):
    taken, (keep_ref, send_ref, acc_ref, h_ref, buf_ref, sems) = rest[:-6], rest[-6:]
    width = w_ref.shape[1]
    start = bounds[0]
    copies = [
        pltpu.make_async_copy(w_ref.at[pl.ds(a, b - a), :], buf_ref.at[pl.ds(a - start, b - a), :], sems.at[k])
        for k, (a, b) in enumerate(zip(bounds, bounds[1:]))
    ]
    for copy in copies:
        copy.start()
    v = g_ref[...] + g2_ref[...].astype(f32)
    h_ref[...] = (v / (1.0 + jnp.exp(-v)) * (u_ref[...] + u2_ref[...].astype(f32))).astype(bf16)
    rows = keep_ref.shape[0]
    passes = [(copy, [(buf_ref, a - start, a, b)]) for copy, a, b in zip(copies, bounds, bounds[1:])]
    if taken:
        place, parts = 0, []
        for ref in taken:
            parts.append((ref, 0, place, place + ref.shape[0]))
            place += ref.shape[0]
        passes.insert(0, (None, parts))
    for k, (copy, parts) in enumerate(passes):
        if copy is not None:
            copy.wait()
        for c in range(0, width, 512):
            total = acc_ref[:, c : c + 512] if k else None
            for ref, at, a, b in parts:
                part = jnp.dot(h_ref[:, a:b], ref[at : at + b - a, c : c + 512], preferred_element_type=f32)
                total = part if total is None else total + part
            if k < len(passes) - 1:
                acc_ref[:, c : c + 512] = total
            else:
                keep_ref[:, c : c + 512] = total[:rows]
                send_ref[:, c : c + 512] = total[rows:].astype(send_ref.dtype)


def add_kernel(a_ref, b_ref, keep_ref, send_ref):
    rows = keep_ref.shape[0]
    total = a_ref[...] + b_ref[...].astype(f32)
    keep_ref[...] = total[:rows]
    send_ref[...] = total[rows:].astype(send_ref.dtype)


def last_kernel(a_ref, b_ref, out_ref):
    out_ref[...] = (a_ref[...] + b_ref[...].astype(f32)).astype(bf16)


def cross(x, groups, mask):
    return lax.ppermute(
        x, ("gx", "gy"), [(2 * i + c, 2 * (i ^ mask) + 1 - c) for i in range(groups) for c in range(2)]
    )


def swap(x, axis, size, mask):
    return lax.ppermute(x, axis, [(i, i ^ mask) for i in range(size)])


def body(tokens, norm_gain, gate_weight, up_weight, down_weight):
    steps, local, half = tokens.shape
    groups, halves = lax.axis_size("gx"), lax.axis_size("gy")
    units = gate_weight.shape[1]
    own_rows = steps * local
    rows = own_rows * groups
    masks = [1 << k for k in range(groups.bit_length() - 1)]
    x = tokens.reshape(own_rows, half)

    pads = (call(empty_kernel, Shape(PAD, f32)),) * PADS
    mark = call(mark_kernel, Shape((8, 128), f32), pads=pads)
    packed = call(pack_kernel, Shape((own_rows + 1, half), f32), mark, x, norm_gain.reshape(1, half))
    own, other = call(
        norm_kernel, (Shape((own_rows, half), bf16),) * 2, packed, swap(packed, "gy", halves, 1)
    )
    held = call(join_kernel, Shape((2 * own_rows, half), bf16), own, cross(other, groups, masks[-1]))
    for mask in reversed(masks[:-1]):
        held = call(join_kernel, Shape((2 * held.shape[0], half), bf16), held, swap(held, "gx", groups, mask))
    down_weight = pltpu.with_memory_space_constraint(down_weight, pltpu.HBM)
    chunk = max(c for c in range(16, 257, 16) if units % c == 0)
    count = units // chunk
    counts = (count * UP_SHARE // 13, count * GATE_SHARE // 13)
    counts = (*counts, count - sum(counts))

    def project(weight, first, ahead, narrow=None):
        outs = [Shape((rows, units), f32)]
        if narrow is not None:
            outs.append(Shape((rows, units), narrow))
        scratch = []
        if ahead:
            outs.append(Shape((ahead * chunk, half), bf16))
            scratch.append(pltpu.SemaphoreType.DMA)
        return call(
            functools.partial(project_kernel, narrow, ahead, chunk, first),
            outs, held, weight, down_weight,
            specs=[VMEM, VMEM, HBM], scratch=scratch, flops=2 * rows * weight.size,
        )

    up, *taken_up = project(up_weight, 0, counts[0])
    up_other = swap(up, "gy", halves, 1)
    gate, gate_send, *taken_gate = project(gate_weight, counts[0], counts[1], bf16)
    gate_other = swap(gate_send, "gy", halves, 1)
    taken = (*taken_up, *taken_gate)
    start = sum(counts[:-1]) * chunk
    bounds = [start]
    while bounds[-1] < units:
        left = units - bounds[-1]
        step = 2 * chunk if left > 3 * chunk else chunk
        if left <= chunk and chunk % 256 == 0:
            step = chunk // 2
        bounds.append(bounds[-1] + min(step, left))
    keep, send = call(
        functools.partial(down_kernel, bounds),
        (Shape((rows // 2, half), f32), Shape((rows // 2, half), bf16)),
        gate, gate_other, up, up_other, down_weight, *taken,
        specs=[VMEM] * 4 + [HBM] + [VMEM] * len(taken),
        scratch=[
            pltpu.VMEM((rows, half), f32),
            pltpu.VMEM((rows, units), bf16),
            pltpu.VMEM((units - start, half), bf16),
            pltpu.SemaphoreType.DMA((len(bounds) - 1,)),
        ],
        limit=DOWN_LIMIT, flops=2 * rows * down_weight.size,
    )
    for mask in masks[:-1]:
        parts = (Shape((keep.shape[0] // 2, half), f32), Shape((keep.shape[0] // 2, half), bf16))
        keep, send = call(add_kernel, parts, keep, swap(send, "gx", groups, mask))
    out = call(last_kernel, Shape((own_rows, half), bf16), keep, swap(send, "gx", groups, masks[-1]))
    return out.reshape(steps, local, half)


def solution(mesh):
    placed = (P(None, ("grp", "gx"), "gy"), P("gy"), P("gy", "gx"), P("gy", "gx"), P("gx", "gy"))
    return jax.shard_map(
        body, mesh=mesh, in_specs=placed, out_specs=P(None, ("grp", "gx"), "gy"), check_vma=False
    )
```

```python
import functools

import jax
import jax.numpy as jnp
from jax import lax
from jax.experimental import pallas as pl
from jax.experimental.pallas import tpu as pltpu
from jax.sharding import PartitionSpec as P

epsilon = 1e-05
f32, bf16 = jnp.float32, jnp.bfloat16
MiB = 2**20
VMEM = pl.BlockSpec(memory_space=pltpu.VMEM)
HBM = pl.BlockSpec(memory_space=pl.ANY)
Shape = jax.ShapeDtypeStruct

PAD = (512, 1024)
PADS = 96
UP_SHARE, GATE_SHARE = 2, 6
DOWN_LIMIT = 13


def call(kernel, outs, *args, pads=(), specs=None, scratch=(), limit=0, flops=0):
    skip = len(pads)
    specs = specs or [VMEM] * len(args)
    limit = max(limit, 2, *(a.shape[0] // 8 for a in args if a.shape[0] <= 256))
    return pl.pallas_call(
        lambda *refs: kernel(*refs[skip:]),
        out_shape=outs,
        in_specs=[VMEM] * skip + specs,
        out_specs=jax.tree.map(lambda _: VMEM, outs),
        scratch_shapes=scratch,
        cost_estimate=pl.CostEstimate(flops=flops, bytes_accessed=flops // 16, transcendentals=0),
        compiler_params=pltpu.CompilerParams(vmem_limit_bytes=limit * MiB),
    )(*pads, *args)


def empty_kernel(out_ref):
    pass


def mark_kernel(out_ref):
    out_ref[...] = jnp.zeros_like(out_ref)


def pack_kernel(mark_ref, x_ref, gain_ref, out_ref):
    rows = x_ref.shape[0]
    out_ref[:rows, :] = x_ref[...].astype(f32)
    out_ref[rows:, :] = gain_ref[...]


def norm_kernel(own_ref, other_ref, own_out_ref, other_out_ref):
    rows = own_out_ref.shape[0]
    halves = [ref[:rows, :] for ref in (own_ref, other_ref)]
    features = 2 * own_ref.shape[1]
    mean_square = sum(jnp.sum(x * x, axis=1, keepdims=True) for x in halves) / features
    scale = lax.rsqrt(mean_square + epsilon)
    for x, ref, out_ref in zip(halves, (own_ref, other_ref), (own_out_ref, other_out_ref)):
        out_ref[...] = (x * scale * ref[rows:, :]).astype(bf16)


def join_kernel(first_ref, second_ref, out_ref):
    rows = first_ref.shape[0]
    out_ref[:rows, :] = first_ref[...]
    out_ref[rows:, :] = second_ref[...]


def project_kernel(narrow, ahead, chunk, first, x_ref, w_ref, down_ref, out_ref, *rest):
    copies = []
    send_ref = None if narrow is None else rest[0]
    if ahead:
        taken_ref, sem = rest[-2:]
        copies.append(pltpu.make_async_copy(down_ref.at[pl.ds(first * chunk, ahead * chunk), :], taken_ref, sem))
        copies[-1].start()
    columns = w_ref.shape[1]
    for c in range(0, columns, 256):
        e = min(c + 256, columns)
        part = jnp.dot(x_ref[...], w_ref[:, c:e], preferred_element_type=f32)
        out_ref[:, c:e] = part
        if send_ref is not None:
            send_ref[:, c:e] = part.astype(narrow)
    for copy in copies:
        copy.wait()


def down_kernel(bounds, g_ref, g2_ref, u_ref, u2_ref, w_ref, *rest):
    taken, (keep_ref, send_ref, acc_ref, h_ref, buf_ref, sems) = rest[:-6], rest[-6:]
    width = w_ref.shape[1]
    start = bounds[0]
    copies = [
        pltpu.make_async_copy(w_ref.at[pl.ds(a, b - a), :], buf_ref.at[pl.ds(a - start, b - a), :], sems.at[k])
        for k, (a, b) in enumerate(zip(bounds, bounds[1:]))
    ]
    for copy in copies:
        copy.start()
    v = g_ref[...] + g2_ref[...].astype(f32)
    h_ref[...] = (v / (1.0 + jnp.exp(-v)) * (u_ref[...] + u2_ref[...].astype(f32))).astype(bf16)
    rows = keep_ref.shape[0]
    passes = [(copy, [(buf_ref, a - start, a, b)]) for copy, a, b in zip(copies, bounds, bounds[1:])]
    if taken:
        place, parts = 0, []
        for ref in taken:
            parts.append((ref, 0, place, place + ref.shape[0]))
            place += ref.shape[0]
        passes.insert(0, (None, parts))
    for k, (copy, parts) in enumerate(passes):
        if copy is not None:
            copy.wait()
        for c in range(0, width, 512):
            total = acc_ref[:, c : c + 512] if k else None
            for ref, at, a, b in parts:
                part = jnp.dot(h_ref[:, a:b], ref[at : at + b - a, c : c + 512], preferred_element_type=f32)
                total = part if total is None else total + part
            if k < len(passes) - 1:
                acc_ref[:, c : c + 512] = total
            else:
                keep_ref[:, c : c + 512] = total[:rows]
                send_ref[:, c : c + 512] = total[rows:].astype(send_ref.dtype)


def add_kernel(a_ref, b_ref, keep_ref, send_ref):
    rows = keep_ref.shape[0]
    total = a_ref[...] + b_ref[...].astype(f32)
    keep_ref[...] = total[:rows]
    send_ref[...] = total[rows:].astype(send_ref.dtype)


def last_kernel(a_ref, b_ref, out_ref):
    out_ref[...] = (a_ref[...] + b_ref[...].astype(f32)).astype(bf16)


def cross(x, groups, mask):
    return lax.ppermute(
        x, ("gx", "gy"), [(2 * i + c, 2 * (i ^ mask) + 1 - c) for i in range(groups) for c in range(2)]
    )


def swap(x, axis, size, mask):
    return lax.ppermute(x, axis, [(i, i ^ mask) for i in range(size)])


def body(tokens, norm_gain, gate_weight, up_weight, down_weight):
    steps, local, half = tokens.shape
    groups, halves = lax.axis_size("gx"), lax.axis_size("gy")
    units = gate_weight.shape[1]
    own_rows = steps * local
    rows = own_rows * groups
    masks = [1 << k for k in range(groups.bit_length() - 1)]
    x = tokens.reshape(own_rows, half)

    pads = (call(empty_kernel, Shape(PAD, f32)),) * PADS
    mark = call(mark_kernel, Shape((8, 128), f32), pads=pads)
    packed = call(pack_kernel, Shape((own_rows + 1, half), f32), mark, x, norm_gain.reshape(1, half))
    own, other = call(
        norm_kernel, (Shape((own_rows, half), bf16),) * 2, packed, swap(packed, "gy", halves, 1)
    )
    held = call(join_kernel, Shape((2 * own_rows, half), bf16), own, cross(other, groups, masks[-1]))
    for mask in reversed(masks[:-1]):
        held = call(join_kernel, Shape((2 * held.shape[0], half), bf16), held, swap(held, "gx", groups, mask))
    down_weight = pltpu.with_memory_space_constraint(down_weight, pltpu.HBM)
    chunk = max(c for c in range(16, 257, 16) if units % c == 0)
    count = units // chunk
    counts = (count * UP_SHARE // 13, count * GATE_SHARE // 13)
    counts = (*counts, count - sum(counts))

    def project(weight, first, ahead, narrow=None):
        outs = [Shape((rows, units), f32)]
        if narrow is not None:
            outs.append(Shape((rows, units), narrow))
        scratch = []
        if ahead:
            outs.append(Shape((ahead * chunk, half), bf16))
            scratch.append(pltpu.SemaphoreType.DMA)
        return call(
            functools.partial(project_kernel, narrow, ahead, chunk, first),
            outs, held, weight, down_weight,
            specs=[VMEM, VMEM, HBM], scratch=scratch, flops=2 * rows * weight.size,
        )

    up, *taken_up = project(up_weight, 0, counts[0])
    up_other = swap(up, "gy", halves, 1)
    gate, gate_send, *taken_gate = project(gate_weight, counts[0], counts[1], bf16)
    gate_other = swap(gate_send, "gy", halves, 1)
    taken = (*taken_up, *taken_gate)
    start = sum(counts[:-1]) * chunk
    bounds = [start]
    while bounds[-1] < units:
        left = units - bounds[-1]
        step = 2 * chunk if left > 3 * chunk else chunk
        if left <= chunk and chunk % 256 == 0:
            step = chunk // 2
        bounds.append(bounds[-1] + min(step, left))
    keep, send = call(
        functools.partial(down_kernel, bounds),
        (Shape((rows // 2, half), f32), Shape((rows // 2, half), bf16)),
        gate, gate_other, up, up_other, down_weight, *taken,
        specs=[VMEM] * 4 + [HBM] + [VMEM] * len(taken),
        scratch=[
            pltpu.VMEM((rows, half), f32),
            pltpu.VMEM((rows, units), bf16),
            pltpu.VMEM((units - start, half), bf16),
            pltpu.SemaphoreType.DMA((len(bounds) - 1,)),
        ],
        limit=DOWN_LIMIT, flops=2 * rows * down_weight.size,
    )
    for mask in masks[:-1]:
        parts = (Shape((keep.shape[0] // 2, half), f32), Shape((keep.shape[0] // 2, half), bf16))
        keep, send = call(add_kernel, parts, keep, swap(send, "gx", groups, mask))
    out = call(last_kernel, Shape((own_rows, half), bf16), keep, swap(send, "gx", groups, masks[-1]))
    return out.reshape(steps, local, half)


def solution(mesh):
    placed = (P(None, ("grp", "gx"), "gy"), P("gy"), P("gy", "gx"), P("gy", "gx"), P("gx", "gy"))
    return jax.shard_map(
        body, mesh=mesh, in_specs=placed, out_specs=P(None, ("grp", "gx"), "gy"), check_vma=False
    )
```

```python
import functools

import jax
import jax.numpy as jnp
from jax import lax
from jax.experimental import pallas as pl
from jax.experimental.pallas import tpu as pltpu
from jax.sharding import PartitionSpec as P

epsilon = 1e-05
f32, bf16 = jnp.float32, jnp.bfloat16
MiB = 2**20
VMEM = pl.BlockSpec(memory_space=pltpu.VMEM)
HBM = pl.BlockSpec(memory_space=pl.ANY)
Shape = jax.ShapeDtypeStruct

PAD = (512, 1024)
PADS = 96
UP_SHARE, GATE_SHARE = 4, 11
DOWN_LIMIT = 14


def call(kernel, outs, *args, pads=(), specs=None, scratch=(), limit=0, flops=0):
    skip = len(pads)
    specs = specs or [VMEM] * len(args)
    limit = max(limit, 2, *(a.shape[0] // 8 for a in args if a.shape[0] <= 256))
    return pl.pallas_call(
        lambda *refs: kernel(*refs[skip:]),
        out_shape=outs,
        in_specs=[VMEM] * skip + specs,
        out_specs=jax.tree.map(lambda _: VMEM, outs),
        scratch_shapes=scratch,
        cost_estimate=pl.CostEstimate(flops=flops, bytes_accessed=flops // 16, transcendentals=0),
        compiler_params=pltpu.CompilerParams(vmem_limit_bytes=limit * MiB),
    )(*pads, *args)


def empty_kernel(out_ref):
    pass


def mark_kernel(out_ref):
    out_ref[...] = jnp.zeros_like(out_ref)


def pack_kernel(mark_ref, x_ref, gain_ref, out_ref):
    rows = x_ref.shape[0]
    out_ref[:rows, :] = x_ref[...].astype(f32)
    out_ref[rows:, :] = gain_ref[...]


def norm_kernel(own_ref, other_ref, own_out_ref, other_out_ref):
    rows = own_out_ref.shape[0]
    halves = [ref[:rows, :] for ref in (own_ref, other_ref)]
    features = 2 * own_ref.shape[1]
    mean_square = sum(jnp.sum(x * x, axis=1, keepdims=True) for x in halves) / features
    scale = lax.rsqrt(mean_square + epsilon)
    for x, ref, out_ref in zip(halves, (own_ref, other_ref), (own_out_ref, other_out_ref)):
        out_ref[...] = (x * scale * ref[rows:, :]).astype(bf16)


def join_kernel(first_ref, second_ref, out_ref):
    rows = first_ref.shape[0]
    out_ref[:rows, :] = first_ref[...]
    out_ref[rows:, :] = second_ref[...]


def project_kernel(narrow, ahead, chunk, first, x_ref, w_ref, down_ref, out_ref, *rest):
    copies = []
    send_ref = None if narrow is None else rest[0]
    if ahead:
        taken_ref, sem = rest[-2:]
        copies.append(pltpu.make_async_copy(down_ref.at[pl.ds(first * chunk, ahead * chunk), :], taken_ref, sem))
        copies[-1].start()
    columns = w_ref.shape[1]
    for c in range(0, columns, 256):
        e = min(c + 256, columns)
        part = jnp.dot(x_ref[...], w_ref[:, c:e], preferred_element_type=f32)
        out_ref[:, c:e] = part
        if send_ref is not None:
            send_ref[:, c:e] = part.astype(narrow)
    for copy in copies:
        copy.wait()


def down_kernel(bounds, g_ref, g2_ref, u_ref, u2_ref, w_ref, *rest):
    taken, (keep_ref, send_ref, acc_ref, h_ref, buf_ref, sems) = rest[:-6], rest[-6:]
    width = w_ref.shape[1]
    start = bounds[0]
    copies = [
        pltpu.make_async_copy(w_ref.at[pl.ds(a, b - a), :], buf_ref.at[pl.ds(a - start, b - a), :], sems.at[k])
        for k, (a, b) in enumerate(zip(bounds, bounds[1:]))
    ]
    for copy in copies:
        copy.start()
    v = g_ref[...] + g2_ref[...].astype(f32)
    h_ref[...] = (v / (1.0 + jnp.exp(-v)) * (u_ref[...] + u2_ref[...].astype(f32))).astype(bf16)
    rows = keep_ref.shape[0]
    passes = [(copy, [(buf_ref, a - start, a, b)]) for copy, a, b in zip(copies, bounds, bounds[1:])]
    if taken:
        place, parts = 0, []
        for ref in taken:
            parts.append((ref, 0, place, place + ref.shape[0]))
            place += ref.shape[0]
        passes.insert(0, (None, parts))
    for k, (copy, parts) in enumerate(passes):
        if copy is not None:
            copy.wait()
        for c in range(0, width, 512):
            total = acc_ref[:, c : c + 512] if k else None
            for ref, at, a, b in parts:
                part = jnp.dot(h_ref[:, a:b], ref[at : at + b - a, c : c + 512], preferred_element_type=f32)
                total = part if total is None else total + part
            if k < len(passes) - 1:
                acc_ref[:, c : c + 512] = total
            else:
                keep_ref[:, c : c + 512] = total[:rows]
                send_ref[:, c : c + 512] = total[rows:].astype(send_ref.dtype)


def add_kernel(a_ref, b_ref, keep_ref, send_ref):
    rows = keep_ref.shape[0]
    total = a_ref[...] + b_ref[...].astype(f32)
    keep_ref[...] = total[:rows]
    send_ref[...] = total[rows:].astype(send_ref.dtype)


def last_kernel(a_ref, b_ref, out_ref):
    out_ref[...] = (a_ref[...] + b_ref[...].astype(f32)).astype(bf16)


def cross(x, groups, mask):
    return lax.ppermute(
        x, ("gx", "gy"), [(2 * i + c, 2 * (i ^ mask) + 1 - c) for i in range(groups) for c in range(2)]
    )


def swap(x, axis, size, mask):
    return lax.ppermute(x, axis, [(i, i ^ mask) for i in range(size)])


def body(tokens, norm_gain, gate_weight, up_weight, down_weight):
    steps, local, half = tokens.shape
    groups, halves = lax.axis_size("gx"), lax.axis_size("gy")
    units = gate_weight.shape[1]
    own_rows = steps * local
    rows = own_rows * groups
    masks = [1 << k for k in range(groups.bit_length() - 1)]
    x = tokens.reshape(own_rows, half)

    pads = (call(empty_kernel, Shape(PAD, f32)),) * PADS
    mark = call(mark_kernel, Shape((8, 128), f32), pads=pads)
    packed = call(pack_kernel, Shape((own_rows + 1, half), f32), mark, x, norm_gain.reshape(1, half))
    own, other = call(
        norm_kernel, (Shape((own_rows, half), bf16),) * 2, packed, swap(packed, "gy", halves, 1)
    )
    held = call(join_kernel, Shape((2 * own_rows, half), bf16), own, cross(other, groups, masks[-1]))
    for mask in reversed(masks[:-1]):
        held = call(join_kernel, Shape((2 * held.shape[0], half), bf16), held, swap(held, "gx", groups, mask))
    down_weight = pltpu.with_memory_space_constraint(down_weight, pltpu.HBM)
    chunk = max(c for c in range(16, 129, 16) if units % c == 0)
    count = units // chunk
    counts = (count * UP_SHARE // 26, count * GATE_SHARE // 26)
    counts = (*counts, count - sum(counts))

    def project(weight, first, ahead, narrow=None):
        outs = [Shape((rows, units), f32)]
        if narrow is not None:
            outs.append(Shape((rows, units), narrow))
        scratch = []
        if ahead:
            outs.append(Shape((ahead * chunk, half), bf16))
            scratch.append(pltpu.SemaphoreType.DMA)
        return call(
            functools.partial(project_kernel, narrow, ahead, chunk, first),
            outs, held, weight, down_weight,
            specs=[VMEM, VMEM, HBM], scratch=scratch, flops=2 * rows * weight.size,
        )

    up, *taken_up = project(up_weight, 0, counts[0])
    up_other = swap(up, "gy", halves, 1)
    gate, gate_send, *taken_gate = project(gate_weight, counts[0], counts[1], bf16)
    gate_other = swap(gate_send, "gy", halves, 1)
    taken = (*taken_up, *taken_gate)
    start = sum(counts[:-1]) * chunk
    bounds = [start]
    while bounds[-1] < units:
        left = units - bounds[-1]
        step = 2 * chunk if left > 3 * chunk else chunk
        if left <= chunk and chunk % 256 == 0:
            step = chunk // 2
        bounds.append(bounds[-1] + min(step, left))
    keep, send = call(
        functools.partial(down_kernel, bounds),
        (Shape((rows // 2, half), f32), Shape((rows // 2, half), bf16)),
        gate, gate_other, up, up_other, down_weight, *taken,
        specs=[VMEM] * 4 + [HBM] + [VMEM] * len(taken),
        scratch=[
            pltpu.VMEM((rows, half), f32),
            pltpu.VMEM((rows, units), bf16),
            pltpu.VMEM((units - start, half), bf16),
            pltpu.SemaphoreType.DMA((len(bounds) - 1,)),
        ],
        limit=DOWN_LIMIT, flops=2 * rows * down_weight.size,
    )
    for mask in masks[:-1]:
        parts = (Shape((keep.shape[0] // 2, half), f32), Shape((keep.shape[0] // 2, half), bf16))
        keep, send = call(add_kernel, parts, keep, swap(send, "gx", groups, mask))
    out = call(last_kernel, Shape((own_rows, half), bf16), keep, swap(send, "gx", groups, masks[-1]))
    return out.reshape(steps, local, half)


def solution(mesh):
    placed = (P(None, ("grp", "gx"), "gy"), P("gy"), P("gy", "gx"), P("gy", "gx"), P("gx", "gy"))
    return jax.shard_map(
        body, mesh=mesh, in_specs=placed, out_specs=P(None, ("grp", "gx"), "gy"), check_vma=False
    )
```

```python
import functools

import jax
import jax.numpy as jnp
from jax import lax
from jax.experimental import pallas as pl
from jax.experimental.pallas import tpu as pltpu
from jax.sharding import PartitionSpec as P

epsilon = 1e-05
f32, bf16 = jnp.float32, jnp.bfloat16
MiB = 2**20
VMEM = pl.BlockSpec(memory_space=pltpu.VMEM)
HBM = pl.BlockSpec(memory_space=pl.ANY)
Shape = jax.ShapeDtypeStruct

PAD = (512, 1024)
PADS = 96
UP_SHARE, GATE_SHARE = 2, 5
DOWN_LIMIT = 15


def call(kernel, outs, *args, pads=(), specs=None, scratch=(), limit=0, flops=0):
    skip = len(pads)
    specs = specs or [VMEM] * len(args)
    limit = max(limit, 2, *(a.shape[0] // 8 for a in args if a.shape[0] <= 256))
    return pl.pallas_call(
        lambda *refs: kernel(*refs[skip:]),
        out_shape=outs,
        in_specs=[VMEM] * skip + specs,
        out_specs=jax.tree.map(lambda _: VMEM, outs),
        scratch_shapes=scratch,
        cost_estimate=pl.CostEstimate(flops=flops, bytes_accessed=flops // 16, transcendentals=0),
        compiler_params=pltpu.CompilerParams(vmem_limit_bytes=limit * MiB),
    )(*pads, *args)


def empty_kernel(out_ref):
    pass


def mark_kernel(out_ref):
    out_ref[...] = jnp.zeros_like(out_ref)


def pack_kernel(mark_ref, x_ref, gain_ref, out_ref):
    rows = x_ref.shape[0]
    out_ref[:rows, :] = x_ref[...].astype(f32)
    out_ref[rows:, :] = gain_ref[...]


def norm_kernel(own_ref, other_ref, own_out_ref, other_out_ref):
    rows = own_out_ref.shape[0]
    halves = [ref[:rows, :] for ref in (own_ref, other_ref)]
    features = 2 * own_ref.shape[1]
    mean_square = sum(jnp.sum(x * x, axis=1, keepdims=True) for x in halves) / features
    scale = lax.rsqrt(mean_square + epsilon)
    for x, ref, out_ref in zip(halves, (own_ref, other_ref), (own_out_ref, other_out_ref)):
        out_ref[...] = (x * scale * ref[rows:, :]).astype(bf16)


def join_kernel(first_ref, second_ref, out_ref):
    rows = first_ref.shape[0]
    out_ref[:rows, :] = first_ref[...]
    out_ref[rows:, :] = second_ref[...]


def project_kernel(narrow, ahead, chunk, first, x_ref, w_ref, down_ref, out_ref, *rest):
    copies = []
    send_ref = None if narrow is None else rest[0]
    if ahead:
        taken_ref, sem = rest[-2:]
        copies.append(pltpu.make_async_copy(down_ref.at[pl.ds(first * chunk, ahead * chunk), :], taken_ref, sem))
        copies[-1].start()
    columns = w_ref.shape[1]
    for c in range(0, columns, 256):
        e = min(c + 256, columns)
        part = jnp.dot(x_ref[...], w_ref[:, c:e], preferred_element_type=f32)
        out_ref[:, c:e] = part
        if send_ref is not None:
            send_ref[:, c:e] = part.astype(narrow)
    for copy in copies:
        copy.wait()


def down_kernel(bounds, g_ref, g2_ref, u_ref, u2_ref, w_ref, *rest):
    taken, (keep_ref, send_ref, acc_ref, h_ref, buf_ref, sems) = rest[:-6], rest[-6:]
    width = w_ref.shape[1]
    start = bounds[0]
    copies = [
        pltpu.make_async_copy(w_ref.at[pl.ds(a, b - a), :], buf_ref.at[pl.ds(a - start, b - a), :], sems.at[k])
        for k, (a, b) in enumerate(zip(bounds, bounds[1:]))
    ]
    for copy in copies:
        copy.start()
    v = g_ref[...] + g2_ref[...].astype(f32)
    h_ref[...] = (v / (1.0 + jnp.exp(-v)) * (u_ref[...] + u2_ref[...].astype(f32))).astype(bf16)
    rows = keep_ref.shape[0]
    passes = [(copy, [(buf_ref, a - start, a, b)]) for copy, a, b in zip(copies, bounds, bounds[1:])]
    if taken:
        place, parts = 0, []
        for ref in taken:
            parts.append((ref, 0, place, place + ref.shape[0]))
            place += ref.shape[0]
        passes.insert(0, (None, parts))
    for k, (copy, parts) in enumerate(passes):
        if copy is not None:
            copy.wait()
        for c in range(0, width, 512):
            total = acc_ref[:, c : c + 512] if k else None
            for ref, at, a, b in parts:
                part = jnp.dot(h_ref[:, a:b], ref[at : at + b - a, c : c + 512], preferred_element_type=f32)
                total = part if total is None else total + part
            if k < len(passes) - 1:
                acc_ref[:, c : c + 512] = total
            else:
                keep_ref[:, c : c + 512] = total[:rows]
                send_ref[:, c : c + 512] = total[rows:].astype(send_ref.dtype)


def add_kernel(a_ref, b_ref, keep_ref, send_ref):
    rows = keep_ref.shape[0]
    total = a_ref[...] + b_ref[...].astype(f32)
    keep_ref[...] = total[:rows]
    send_ref[...] = total[rows:].astype(send_ref.dtype)


def last_kernel(a_ref, b_ref, out_ref):
    out_ref[...] = (a_ref[...] + b_ref[...].astype(f32)).astype(bf16)


def cross(x, groups, mask):
    return lax.ppermute(
        x, ("gx", "gy"), [(2 * i + c, 2 * (i ^ mask) + 1 - c) for i in range(groups) for c in range(2)]
    )


def swap(x, axis, size, mask):
    return lax.ppermute(x, axis, [(i, i ^ mask) for i in range(size)])


def body(tokens, norm_gain, gate_weight, up_weight, down_weight):
    steps, local, half = tokens.shape
    groups, halves = lax.axis_size("gx"), lax.axis_size("gy")
    units = gate_weight.shape[1]
    own_rows = steps * local
    rows = own_rows * groups
    masks = [1 << k for k in range(groups.bit_length() - 1)]
    masks = [*masks[1:2], *masks[:1], *masks[2:]]
    x = tokens.reshape(own_rows, half)

    pads = (call(empty_kernel, Shape(PAD, f32)),) * PADS
    mark = call(mark_kernel, Shape((8, 128), f32), pads=pads)
    packed = call(pack_kernel, Shape((own_rows + 1, half), f32), mark, x, norm_gain.reshape(1, half))
    own, other = call(
        norm_kernel, (Shape((own_rows, half), bf16),) * 2, packed, swap(packed, "gy", halves, 1)
    )
    held = call(join_kernel, Shape((2 * own_rows, half), bf16), own, cross(other, groups, masks[-1]))
    for mask in reversed(masks[:-1]):
        held = call(join_kernel, Shape((2 * held.shape[0], half), bf16), held, swap(held, "gx", groups, mask))
    down_weight = pltpu.with_memory_space_constraint(down_weight, pltpu.HBM)
    chunk = max(c for c in range(16, 257, 16) if units % c == 0)
    count = units // chunk
    counts = (count * UP_SHARE // 13, count * GATE_SHARE // 13)
    counts = (*counts, count - sum(counts))

    def project(weight, first, ahead, narrow=None):
        outs = [Shape((rows, units), f32)]
        if narrow is not None:
            outs.append(Shape((rows, units), narrow))
        scratch = []
        if ahead:
            outs.append(Shape((ahead * chunk, half), bf16))
            scratch.append(pltpu.SemaphoreType.DMA)
        return call(
            functools.partial(project_kernel, narrow, ahead, chunk, first),
            outs, held, weight, down_weight,
            specs=[VMEM, VMEM, HBM], scratch=scratch, flops=2 * rows * weight.size,
        )

    up, *taken_up = project(up_weight, 0, counts[0])
    up_other = swap(up, "gy", halves, 1)
    gate, gate_send, *taken_gate = project(gate_weight, counts[0], counts[1], bf16)
    gate_other = swap(gate_send, "gy", halves, 1)
    taken = (*taken_up, *taken_gate)
    start = sum(counts[:-1]) * chunk
    bounds = [start]
    while bounds[-1] < units:
        left = units - bounds[-1]
        step = 2 * chunk if left > 3 * chunk else chunk
        if left <= chunk and chunk % 256 == 0:
            step = chunk // 2
        bounds.append(bounds[-1] + min(step, left))
    keep, send = call(
        functools.partial(down_kernel, bounds),
        (Shape((rows // 2, half), f32), Shape((rows // 2, half), bf16)),
        gate, gate_other, up, up_other, down_weight, *taken,
        specs=[VMEM] * 4 + [HBM] + [VMEM] * len(taken),
        scratch=[
            pltpu.VMEM((rows, half), f32),
            pltpu.VMEM((rows, units), bf16),
            pltpu.VMEM((units - start, half), bf16),
            pltpu.SemaphoreType.DMA((len(bounds) - 1,)),
        ],
        limit=DOWN_LIMIT, flops=2 * rows * down_weight.size,
    )
    for mask in masks[:-1]:
        parts = (Shape((keep.shape[0] // 2, half), f32), Shape((keep.shape[0] // 2, half), bf16))
        keep, send = call(add_kernel, parts, keep, swap(send, "gx", groups, mask))
    out = call(last_kernel, Shape((own_rows, half), bf16), keep, swap(send, "gx", groups, masks[-1]))
    return out.reshape(steps, local, half)


def solution(mesh):
    placed = (P(None, ("grp", "gx"), "gy"), P("gy"), P("gy", "gx"), P("gy", "gx"), P("gx", "gy"))
    return jax.shard_map(
        body, mesh=mesh, in_specs=placed, out_specs=P(None, ("grp", "gx"), "gy"), check_vma=False
    )
```

```python
import functools

import jax
import jax.numpy as jnp
from jax import lax
from jax.experimental import pallas as pl
from jax.experimental.pallas import tpu as pltpu
from jax.sharding import PartitionSpec as P

epsilon = 1e-05
f32, bf16 = jnp.float32, jnp.bfloat16
MiB = 2**20
VMEM = pl.BlockSpec(memory_space=pltpu.VMEM)
HBM = pl.BlockSpec(memory_space=pl.ANY)
Shape = jax.ShapeDtypeStruct

PAD = (512, 1024)
PADS = 96
UP_SHARE, GATE_SHARE = 2, 5
DOWN_LIMIT = 15


def call(kernel, outs, *args, pads=(), specs=None, scratch=(), limit=0, flops=0):
    skip = len(pads)
    specs = specs or [VMEM] * len(args)
    limit = max(limit, 2, *(a.shape[0] // 8 for a in args if a.shape[0] <= 256))
    return pl.pallas_call(
        lambda *refs: kernel(*refs[skip:]),
        out_shape=outs,
        in_specs=[VMEM] * skip + specs,
        out_specs=jax.tree.map(lambda _: VMEM, outs),
        scratch_shapes=scratch,
        cost_estimate=pl.CostEstimate(flops=flops, bytes_accessed=flops // 16, transcendentals=0),
        compiler_params=pltpu.CompilerParams(vmem_limit_bytes=limit * MiB),
    )(*pads, *args)


def empty_kernel(out_ref):
    pass


def mark_kernel(out_ref):
    out_ref[...] = jnp.zeros_like(out_ref)


def pack_kernel(mark_ref, x_ref, gain_ref, out_ref):
    rows = x_ref.shape[0]
    out_ref[:rows, :] = x_ref[...].astype(f32)
    out_ref[rows:, :] = gain_ref[...]


def norm_kernel(own_ref, other_ref, own_out_ref, other_out_ref):
    rows = own_out_ref.shape[0]
    halves = [ref[:rows, :] for ref in (own_ref, other_ref)]
    features = 2 * own_ref.shape[1]
    mean_square = sum(jnp.sum(x * x, axis=1, keepdims=True) for x in halves) / features
    scale = lax.rsqrt(mean_square + epsilon)
    for x, ref, out_ref in zip(halves, (own_ref, other_ref), (own_out_ref, other_out_ref)):
        out_ref[...] = (x * scale * ref[rows:, :]).astype(bf16)


def join_kernel(first_ref, second_ref, out_ref):
    rows = first_ref.shape[0]
    out_ref[:rows, :] = first_ref[...]
    out_ref[rows:, :] = second_ref[...]


def project_kernel(narrow, ahead, chunk, first, x_ref, w_ref, down_ref, out_ref, *rest):
    copies = []
    send_ref = None if narrow is None else rest[0]
    if ahead:
        taken_ref, sem = rest[-2:]
        copies.append(pltpu.make_async_copy(down_ref.at[pl.ds(first * chunk, ahead * chunk), :], taken_ref, sem))
        copies[-1].start()
    columns = w_ref.shape[1]
    for c in range(0, columns, 256):
        e = min(c + 256, columns)
        part = jnp.dot(x_ref[...], w_ref[:, c:e], preferred_element_type=f32)
        out_ref[:, c:e] = part
        if send_ref is not None:
            send_ref[:, c:e] = part.astype(narrow)
    for copy in copies:
        copy.wait()


def down_kernel(bounds, g_ref, g2_ref, u_ref, u2_ref, w_ref, *rest):
    taken, (keep_ref, send_ref, acc_ref, h_ref, buf_ref, sems) = rest[:-6], rest[-6:]
    width = w_ref.shape[1]
    start = bounds[0]
    copies = [
        pltpu.make_async_copy(w_ref.at[pl.ds(a, b - a), :], buf_ref.at[pl.ds(a - start, b - a), :], sems.at[k])
        for k, (a, b) in enumerate(zip(bounds, bounds[1:]))
    ]
    for copy in copies:
        copy.start()
    v = g_ref[...] + g2_ref[...].astype(f32)
    h_ref[...] = (v / (1.0 + jnp.exp(-v)) * (u_ref[...] + u2_ref[...].astype(f32))).astype(bf16)
    rows = keep_ref.shape[0]
    passes = [(copy, [(buf_ref, a - start, a, b)]) for copy, a, b in zip(copies, bounds, bounds[1:])]
    if taken:
        place, parts = 0, []
        for ref in taken:
            parts.append((ref, 0, place, place + ref.shape[0]))
            place += ref.shape[0]
        passes.insert(0, (None, parts))
    for k, (copy, parts) in enumerate(passes):
        if copy is not None:
            copy.wait()
        for c in range(0, width, 1024):
            total = acc_ref[:, c : c + 1024] if k else None
            for ref, at, a, b in parts:
                part = jnp.dot(h_ref[:, a:b], ref[at : at + b - a, c : c + 1024], preferred_element_type=f32)
                total = part if total is None else total + part
            if k < len(passes) - 1:
                acc_ref[:, c : c + 1024] = total
            else:
                keep_ref[:, c : c + 1024] = total[:rows]
                send_ref[:, c : c + 1024] = total[rows:].astype(send_ref.dtype)


def add_kernel(a_ref, b_ref, keep_ref, send_ref):
    rows = keep_ref.shape[0]
    total = a_ref[...] + b_ref[...].astype(f32)
    keep_ref[...] = total[:rows]
    send_ref[...] = total[rows:].astype(send_ref.dtype)


def last_kernel(a_ref, b_ref, out_ref):
    out_ref[...] = (a_ref[...] + b_ref[...].astype(f32)).astype(bf16)


def cross(x, groups, mask):
    return lax.ppermute(
        x, ("gx", "gy"), [(2 * i + c, 2 * (i ^ mask) + 1 - c) for i in range(groups) for c in range(2)]
    )


def swap(x, axis, size, mask):
    return lax.ppermute(x, axis, [(i, i ^ mask) for i in range(size)])


def body(tokens, norm_gain, gate_weight, up_weight, down_weight):
    steps, local, half = tokens.shape
    groups, halves = lax.axis_size("gx"), lax.axis_size("gy")
    units = gate_weight.shape[1]
    own_rows = steps * local
    rows = own_rows * groups
    masks = [1 << k for k in range(groups.bit_length() - 1)]
    x = tokens.reshape(own_rows, half)

    pads = (call(empty_kernel, Shape(PAD, f32)),) * PADS
    mark = call(mark_kernel, Shape((8, 128), f32), pads=pads)
    packed = call(pack_kernel, Shape((own_rows + 1, half), f32), mark, x, norm_gain.reshape(1, half))
    own, other = call(
        norm_kernel, (Shape((own_rows, half), bf16),) * 2, packed, swap(packed, "gy", halves, 1)
    )
    held = call(join_kernel, Shape((2 * own_rows, half), bf16), own, cross(other, groups, masks[-1]))
    for mask in reversed(masks[:-1]):
        held = call(join_kernel, Shape((2 * held.shape[0], half), bf16), held, swap(held, "gx", groups, mask))
    down_weight = pltpu.with_memory_space_constraint(down_weight, pltpu.HBM)
    chunk = max(c for c in range(16, 257, 16) if units % c == 0)
    count = units // chunk
    counts = (count * UP_SHARE // 13, count * GATE_SHARE // 13)
    counts = (*counts, count - sum(counts))

    def project(weight, first, ahead, narrow=None):
        outs = [Shape((rows, units), f32)]
        if narrow is not None:
            outs.append(Shape((rows, units), narrow))
        scratch = []
        if ahead:
            outs.append(Shape((ahead * chunk, half), bf16))
            scratch.append(pltpu.SemaphoreType.DMA)
        return call(
            functools.partial(project_kernel, narrow, ahead, chunk, first),
            outs, held, weight, down_weight,
            specs=[VMEM, VMEM, HBM], scratch=scratch, flops=2 * rows * weight.size,
        )

    up, *taken_up = project(up_weight, 0, counts[0])
    up_other = swap(up, "gy", halves, 1)
    gate, gate_send, *taken_gate = project(gate_weight, counts[0], counts[1], bf16)
    gate_other = swap(gate_send, "gy", halves, 1)
    taken = (*taken_up, *taken_gate)
    start = sum(counts[:-1]) * chunk
    bounds = [start]
    while bounds[-1] < units:
        left = units - bounds[-1]
        step = 2 * chunk if left > 3 * chunk else chunk
        if left <= chunk and chunk % 256 == 0:
            step = chunk // 2
        bounds.append(bounds[-1] + min(step, left))
    keep, send = call(
        functools.partial(down_kernel, bounds),
        (Shape((rows // 2, half), f32), Shape((rows // 2, half), bf16)),
        gate, gate_other, up, up_other, down_weight, *taken,
        specs=[VMEM] * 4 + [HBM] + [VMEM] * len(taken),
        scratch=[
            pltpu.VMEM((rows, half), f32),
            pltpu.VMEM((rows, units), bf16),
            pltpu.VMEM((units - start, half), bf16),
            pltpu.SemaphoreType.DMA((len(bounds) - 1,)),
        ],
        limit=DOWN_LIMIT, flops=2 * rows * down_weight.size,
    )
    for mask in masks[:-1]:
        parts = (Shape((keep.shape[0] // 2, half), f32), Shape((keep.shape[0] // 2, half), bf16))
        keep, send = call(add_kernel, parts, keep, swap(send, "gx", groups, mask))
    out = call(last_kernel, Shape((own_rows, half), bf16), keep, swap(send, "gx", groups, masks[-1]))
    return out.reshape(steps, local, half)


def solution(mesh):
    placed = (P(None, ("grp", "gx"), "gy"), P("gy"), P("gy", "gx"), P("gy", "gx"), P("gx", "gy"))
    return jax.shard_map(
        body, mesh=mesh, in_specs=placed, out_specs=P(None, ("grp", "gx"), "gy"), check_vma=False
    )
```
